768 devices in a mesh: lat: 12 (over z), lon: 64 (over x, y, core).
Axes of the slice: x: 4, y: 8, z: 12, core: 2. Of those that a mesh axis runs over, the one named last changes fastest.
Arguments:
- fields: float32 [768, 1152, 128], P('lat', 'lon'), may hold values from -6 to 6
- cutoff: int32 [768], replicated, may hold values from 2 to 288
- cap_mask: int32 [768], replicated, may hold values from 0 to 1, as said below
- coef_lon: float32 [768, 1152], P('lat', 'lon'), may hold values from 0.02 to 0.16
- coef_lat: float32 [768, 1152], P('lat', 'lon'), may hold values from 0.02 to 0.16
- coef_vert: float32 [768, 1152], P('lat', 'lon'), may hold values from 0.02 to 0.16
Outputs:
- updated: float32 [768, 1152, 128], P('lat', 'lon')
The draws below stay inside these ranges and needn't reach their ends.
Inputs may be any that keep to these rules, and one draw needn't show every extreme that they name: cap_mask is 1 on the first 96 and the last 96 latitudes, 0 on latitudes 768//4 to 575, and 0 or 1 for each latitude in between.
All inputs are finite; a program needn't handle non-finite values.
Results may differ from the reference program's by a relative error of at most 0.0003.
Values sent between devices are 32-bit elements; how exact they have to be, the bound alone decides.
No kernel may reach another device: no remote copies, remote signals or barrier semaphores. Data moves between devices by JAX's collectives and lax.ppermute only.
A program may use at most 64 MiB of HBM per device.

```python
import math
import jax
import jax.numpy as jnp
from jax import lax

NLON = 1152
NF = 8
LEV = 16
FL = 128
NLAT = 768


def draw_cap_mask(key, part):
    key = jax.random.fold_in(key, 7)
    rows = jnp.arange(NLAT, dtype=jnp.int32)
    distance = jnp.minimum(rows, NLAT - 1 - rows)
    random_bits = jax.random.randint(key, (NLAT,), 0, 2).astype(jnp.int32)
    inner = jnp.where(distance < NLAT // 4, random_bits, 0)
    return jnp.where(distance < NLAT // 8, 1, inner).astype(jnp.int32)


def plant(values, own_key, low, largest):
    longest = values.shape.index(max(values.shape))
    spots = []
    for shift in (0, 1):
        where = [jax.random.randint(jax.random.fold_in(own_key, axis), (), 0, length) for axis, length in enumerate(values.shape)]
        where[longest] = (where[longest] + shift) % values.shape[longest]
        spots.append(tuple(where))
    return values.at[spots[0]].set(low).at[spots[1]].set(largest)


def level_of(rng, shape, cuts, low, largest):
    loudness, own = 1.0, jax.random.fold_in(rng, 6)
    for axis_at, shards_of in cuts:
        heights = jnp.exp(jax.random.uniform(jax.random.fold_in(own, axis_at), (shards_of,), jnp.float32, low / len(cuts), largest / len(cuts)))
        loudness = loudness * jnp.repeat(heights, shape[axis_at] // shards_of).reshape([-1 if axis == axis_at else 1 for axis in range(len(shape))])
    return loudness


def bell_draw(stream_key, shape, scale, reach, pieces=(), held_as=jnp.bfloat16):
    array = scale * jax.random.normal(stream_key, shape, jnp.float32)
    if pieces:
        array = array * level_of(stream_key, shape, pieces, -0.22, 0.18)
    return jnp.clip(array, -reach, reach).astype(held_as)


def setup_inputs(seed: int = 0) -> dict:
    streams_of = jax.random.split(jax.random.key(seed), 7)
    return {
        "fields": bell_draw(streams_of[0], (NLAT, NLON, FL), 1.0, 6.0, ((0, 12), (1, 64)), jnp.float32),
        "cutoff": plant(jax.random.randint(streams_of[1], (NLAT,), 2, NLON // 4 + 1), jax.random.fold_in(streams_of[1], 1), 2, (NLON // 4 + 1) - 1).astype(jnp.int32),
        "cap_mask": draw_cap_mask(jax.random.fold_in(streams_of[6], 71), 0),
        "coef_lon": jnp.clip(jnp.exp(math.log(0.16) - 2.0794415 * jax.random.uniform(streams_of[3], (NLAT, NLON), jnp.float32) ** level_of(streams_of[3], (NLAT, NLON), ((0, 12), (1, 64)), -0.2, 0.2)), 0.02, 0.16),
        "coef_lat": jnp.clip(jnp.exp(math.log(0.16) - 2.0794415 * jax.random.uniform(streams_of[4], (NLAT, NLON), jnp.float32) ** level_of(streams_of[4], (NLAT, NLON), ((0, 12), (1, 64)), -0.2, 0.2)), 0.02, 0.16),
        "coef_vert": jnp.clip(jnp.exp(math.log(0.16) - 2.0794415 * jax.random.uniform(streams_of[5], (NLAT, NLON), jnp.float32) ** level_of(streams_of[5], (NLAT, NLON), ((0, 12), (1, 64)), -0.2, 0.2)), 0.02, 0.16),
    }


def filter_row(args):
    row, cut, cap = args
    spectrum = jnp.fft.rfft(row, axis=0)
    waves = jnp.arange(spectrum.shape[0])
    keep = (waves < cut)[:, None]
    spectrum = jnp.where(keep, spectrum, jnp.zeros_like(spectrum))
    smooth = jnp.fft.irfft(spectrum, n=NLON, axis=0).astype(row.dtype)
    return jnp.where(cap == 1, smooth, row)


def reference(fields, cutoff, cap_mask, coef_lon, coef_lat, coef_vert):
    filtered = lax.map(filter_row, (fields, cutoff, cap_mask))
    columns = jnp.arange(FL) // LEV
    sign = jnp.where(columns < 2, -1.0, 1.0).astype(jnp.float32)
    north = sign * jnp.roll(filtered[0], NLON // 2, axis=0)
    south = sign * jnp.roll(filtered[-1], NLON // 2, axis=0)
    ext = jnp.concatenate([north[None], filtered, south[None]], axis=0)
    east = jnp.roll(filtered, -1, axis=1)
    west = jnp.roll(filtered, 1, axis=1)
    lat_term = ext[2:] + ext[:-2] - 2.0 * filtered
    lon_term = east + west - 2.0 * filtered
    stacked = filtered.reshape(NLAT, NLON, NF, LEV)
    zero = jnp.zeros((NLAT, NLON, NF, 1), jnp.float32)
    above = jnp.concatenate([stacked[..., 1:], zero], axis=3)
    below = jnp.concatenate([zero, stacked[..., :-1]], axis=3)
    vert_term = (above + below - 2.0 * stacked).reshape(NLAT, NLON, FL)
    return filtered + coef_lon[..., None] * lon_term + coef_lat[..., None] * lat_term + coef_vert[..., None] * vert_term
```

```python
import functools

import jax
import jax.numpy as jnp
import ml_dtypes
import numpy as np
from jax import lax
from jax.experimental import pallas as pl
from jax.experimental.pallas import tpu as pltpu
from jax.sharding import PartitionSpec as P

LEV = 16
WAVES = 288


def split_table(table):
    high = table.astype(ml_dtypes.bfloat16)
    low = (table - high.astype(np.float64)).astype(ml_dtypes.bfloat16)
    return np.concatenate([high, low], axis=0)


def tables(full, cols):
    half = full // 2
    sectors = half // cols
    place = (np.arange(cols)[:, None] + cols * np.arange(sectors)[None, :]).reshape(-1)
    made = []
    for parity in (0, 1):
        wave = np.arange(parity, WAVES, 2)
        angle = (wave[:, None] * place[None, :] % full) * (2.0 * np.pi / full)
        made.append(np.concatenate([np.cos(angle), np.sin(angle)], axis=0))
    return [split_table(m) for m in made] + [split_table(m.T) for m in made]


def pack_kernel(x_ref, out_ref):
    cols, rows, _ = x_ref.shape
    for j in range(cols):
        out_ref[pl.ds(j, rows, stride=cols), :] = x_ref[j]


def halves(values):
    high = values.astype(jnp.bfloat16)
    low = (values - high.astype(jnp.float32)).astype(jnp.bfloat16)
    return high, low


def product(table_ref, data):
    both = jnp.dot(table_ref[...], data, preferred_element_type=jnp.float32)
    rows = both.shape[0] // 2
    depth = both.shape[1] // 2
    return (both[:rows, :depth] + both[:rows, depth:]) + (both[rows:, :depth] + both[rows:, depth:])


def filter_kernel(cols, peers, cut_ref, cap_ref, x_ref, fe_ref, fo_ref, be_ref, bo_ref, out_ref, even, odd):
    depth = x_ref.shape[1]
    full = cols * peers
    half = peers // 2
    wide = cols + 2
    row = lax.axis_index("lat") * peers + lax.axis_index("lon")
    cut = cut_ref[row]
    cap = cap_ref[row]

    def emit(j, values):
        out_ref[pl.ds(1 + j, peers, stride=wide), :] = values
        if j == cols - 1:
            out_ref[pl.ds(0, peers, stride=wide), :] = pltpu.roll(values, 1, 0)
        if j == 0:
            out_ref[pl.ds(wide - 1, peers, stride=wide), :] = pltpu.roll(values, peers - 1, 0)

    @pl.when(cap != 1)
    def _():
        for j in range(cols):
            emit(j, x_ref[pl.ds(j, peers, stride=cols), :])

    @pl.when(cap == 1)
    def _():
        for j in range(cols):
            values = x_ref[pl.ds(j, peers, stride=cols), :]
            for ref, folded in ((even, values[:half] + values[half:]), (odd, values[:half] - values[half:])):
                high, low = halves(folded)
                ref[pl.ds(j * half, half), 0:depth] = high
                ref[pl.ds(j * half, half), depth : 2 * depth] = low
        back = []
        for parity, ref, forth_ref, back_ref in ((0, even, fe_ref, be_ref), (1, odd, fo_ref, bo_ref)):
            spectrum = product(forth_ref, ref[...])
            index = lax.broadcasted_iota(jnp.int32, spectrum.shape, 0)
            count = WAVES // 2
            wave = 2 * jnp.where(index < count, index, index - count) + parity
            weight = jnp.where(wave == 0, 1.0 / full, 2.0 / full)
            spectrum = jnp.where(wave < cut, spectrum * weight, 0.0)
            back.append(product(back_ref, jnp.concatenate(halves(spectrum), axis=1)))
        for j in range(cols):
            near = back[0][j * half : (j + 1) * half]
            far = back[1][j * half : (j + 1) * half]
            emit(j, jnp.concatenate([near + far, near - far], axis=0))


def stencil_kernel(cols, rows, n_lat, g_ref, north_ref, south_ref, far_ref, cl_ref, ct_ref, cv_ref, out_ref):
    wide = cols + 2
    depth = g_ref.shape[1]
    lat = lax.axis_index("lat")
    lane = lax.broadcasted_iota(jnp.int32, (rows, depth), 1)
    line = lax.broadcasted_iota(jnp.int32, (rows, depth), 0)
    top = lane % LEV == LEV - 1
    bottom = lane % LEV == 0
    sign = jnp.where(lax.broadcasted_iota(jnp.int32, (cols, depth), 1) < 2 * LEV, -1.0, 1.0)
    north = jnp.where(lat == 0, sign * far_ref[0], north_ref[...])
    south = jnp.where(lat == n_lat - 1, sign * far_ref[1], south_ref[...])
    coefs = [jnp.transpose(ref[...]) for ref in (cl_ref, ct_ref, cv_ref)]
    line_of = [g_ref[pl.ds(i, rows, stride=wide), :] for i in range(2)]
    for j in range(cols):
        line_of.append(g_ref[pl.ds(j + 2, rows, stride=wide), :])
        west, here, east = line_of[j : j + 3]
        up = jnp.where(line == 0, north[j : j + 1], pltpu.roll(here, 1, 0))
        down = jnp.where(line == rows - 1, south[j : j + 1], pltpu.roll(here, rows - 1, 0))
        above = jnp.where(top, 0.0, pltpu.roll(here, depth - 1, 1))
        below = jnp.where(bottom, 0.0, pltpu.roll(here, 1, 1))
        twice = 2.0 * here
        out_ref[j] = (
            here
            + coefs[0][:, j : j + 1] * (east + west - twice)
            + coefs[1][:, j : j + 1] * (up + down - twice)
            + coefs[2][:, j : j + 1] * (above + below - twice)
        )


def per_device(fields, cutoff, cap_mask, coef_lon, coef_lat, coef_vert):
    rows, cols, depth = fields.shape
    peers = lax.axis_size("lon")
    n_lat = lax.axis_size("lat")
    vmem = pl.BlockSpec(memory_space=pltpu.VMEM)
    smem = pl.BlockSpec(memory_space=pltpu.SMEM)
    wide = cols + 2

    packed = pl.pallas_call(
        pack_kernel,
        out_shape=jax.ShapeDtypeStruct((rows * cols, depth), jnp.float32),
        in_specs=[vmem],
        out_specs=vmem,
        name="pack",
    )(jnp.transpose(fields, (1, 0, 2)))
    block = lax.all_to_all(packed.reshape(peers, cols, 1, depth), "lon", 0, 0, tiled=True)
    forth_even, forth_odd, back_even, back_odd = tables(cols * peers, cols)
    half = cols * peers // 2
    filtered = pl.pallas_call(
        functools.partial(filter_kernel, cols, peers),
        out_shape=jax.ShapeDtypeStruct((peers * wide, depth), jnp.float32),
        in_specs=[smem, smem] + [vmem] * 5,
        out_specs=vmem,
        scratch_shapes=[pltpu.VMEM((half, 2 * depth), jnp.bfloat16)] * 2,
        compiler_params=pltpu.CompilerParams(vmem_limit_bytes=24 * 1024 * 1024),
        name="filter",
    )(
        cutoff,
        cap_mask,
        block.reshape(peers * cols, depth),
        jnp.asarray(forth_even),
        jnp.asarray(forth_odd),
        jnp.asarray(back_even),
        jnp.asarray(back_odd),
    )
    returned = lax.all_to_all(filtered.reshape(peers, wide, 1, depth), "lon", 0, 0, tiled=True)
    head = returned[0, 1:-1, 0]
    tail = returned[-1, 1:-1, 0]
    ring = [(i, (i + 1) % n_lat) for i in range(n_lat)]
    north = lax.ppermute(tail, "lat", ring)
    south = lax.ppermute(head, "lat", [(b, a) for a, b in ring])
    far = lax.ppermute(jnp.stack([head, tail]), "lon", [(i, (i + peers // 2) % peers) for i in range(peers)])
    out = pl.pallas_call(
        functools.partial(stencil_kernel, cols, rows, n_lat),
        out_shape=jax.ShapeDtypeStruct((cols, rows, depth), jnp.float32),
        in_specs=[vmem] * 7,
        out_specs=vmem,
        name="stencil",
    )(
        returned.reshape(rows * wide, depth),
        north,
        south,
        far,
        jnp.transpose(coef_lon),
        jnp.transpose(coef_lat),
        jnp.transpose(coef_vert),
    )
    return jnp.transpose(out, (1, 0, 2))


def solution(mesh):
    return jax.shard_map(
        per_device,
        mesh=mesh,
        in_specs=(
            P("lat", "lon", None),
            P(),
            P(),
            P("lat", "lon"),
            P("lat", "lon"),
            P("lat", "lon"),
        ),
        out_specs=P("lat", "lon", None),
        check_vma=False,
    )
```

```python
import functools

import jax
import jax.numpy as jnp
import ml_dtypes
import numpy as np
from jax import lax
from jax.experimental import pallas as pl
from jax.experimental.pallas import tpu as pltpu
from jax.sharding import PartitionSpec as P

LEV = 16
WAVES = 288


def split_table(table):
    high = table.astype(ml_dtypes.bfloat16)
    low = (table - high.astype(np.float64)).astype(ml_dtypes.bfloat16)
    return np.concatenate([high, low], axis=0)


def tables(full, cols):
    half = full // 2
    sectors = half // cols
    place = (np.arange(cols)[:, None] + cols * np.arange(sectors)[None, :]).reshape(-1)
    made = []
    for parity in (0, 1):
        wave = np.arange(parity, WAVES, 2)
        angle = (wave[:, None] * place[None, :] % full) * (2.0 * np.pi / full)
        made.append(np.concatenate([np.cos(angle), np.sin(angle)], axis=0))
    forth = np.concatenate([split_table(m) for m in made], axis=0)
    back = np.concatenate([split_table(m.T) for m in made], axis=0)
    return forth, back


def pack_kernel(x_ref, out_ref, held, sems):
    cols, rows, _ = x_ref.shape
    parts = sems.shape[0]
    size = cols // parts
    copies = []
    for i in range(parts):
        part = pl.ds(i * size, size)
        copies.append(pltpu.make_async_copy(x_ref.at[part], held.at[part], sems.at[i]))
        copies[-1].start()
    for i in range(parts):
        copies[i].wait()
        for j in range(i * size, (i + 1) * size):
            out_ref[pl.ds(j, rows, stride=cols), :] = held[j]


def halves(values):
    high = values.astype(jnp.bfloat16)
    low = (values - high.astype(jnp.float32)).astype(jnp.bfloat16)
    return high, low


def product(table, data):
    both = jnp.dot(table, data, preferred_element_type=jnp.float32)
    rows = both.shape[0] // 2
    depth = both.shape[1] // 2
    return (both[:rows, :depth] + both[:rows, depth:]) + (both[rows:, :depth] + both[rows:, depth:])


def filter_kernel(cols, peers, cut_ref, cap_ref, x_ref, forth_ref, back_ref, out_ref, even, odd):
    depth = x_ref.shape[1]
    full = cols * peers
    half = peers // 2
    wide = cols + 2
    row = lax.axis_index("lat") * peers + lax.axis_index("lon")
    cut = cut_ref[row]
    cap = cap_ref[row]

    def emit(j, values):
        out_ref[pl.ds(1 + j, peers, stride=wide), :] = values
        if j == cols - 1:
            out_ref[pl.ds(0, peers, stride=wide), :] = pltpu.roll(values, 1, 0)
        if j == 0:
            out_ref[pl.ds(wide - 1, peers, stride=wide), :] = pltpu.roll(values, peers - 1, 0)

    @pl.when(cap != 1)
    def _():
        for j in range(cols):
            emit(j, x_ref[pl.ds(j, peers, stride=cols), :])

    @pl.when(cap == 1)
    def _():
        for j in range(cols):
            values = x_ref[pl.ds(j, peers, stride=cols), :]
            for ref, folded in ((even, values[:half] + values[half:]), (odd, values[:half] - values[half:])):
                high, low = halves(folded)
                ref[pl.ds(j * half, half), 0:depth] = high
                ref[pl.ds(j * half, half), depth : 2 * depth] = low
        back = []
        for parity, ref in ((0, even), (1, odd)):
            spectrum = product(forth_ref[pl.ds(parity * 2 * WAVES, 2 * WAVES), :], ref[...])
            index = lax.broadcasted_iota(jnp.int32, spectrum.shape, 0)
            count = WAVES // 2
            wave = 2 * jnp.where(index < count, index, index - count) + parity
            weight = jnp.where(wave == 0, 1.0 / full, 2.0 / full)
            spectrum = jnp.where(wave < cut, spectrum * weight, 0.0)
            table = back_ref[pl.ds(parity * full, full), :]
            back.append(product(table, jnp.concatenate(halves(spectrum), axis=1)))
        for j in range(cols):
            near = back[0][j * half : (j + 1) * half]
            far = back[1][j * half : (j + 1) * half]
            emit(j, jnp.concatenate([near + far, near - far], axis=0))


def stencil_kernel(cols, rows, n_lat, g_ref, first_ref, second_ref, cl_ref, ct_ref, cv_ref, out_ref, made, sems):
    wide = cols + 2
    depth = g_ref.shape[1]
    parts = sems.shape[0]
    size = cols // parts
    lat = lax.axis_index("lat")
    odd = lat % 2 == 1
    lane = lax.broadcasted_iota(jnp.int32, (rows, depth), 1)
    line = lax.broadcasted_iota(jnp.int32, (rows, depth), 0)
    top = lane % LEV == LEV - 1
    bottom = lane % LEV == 0
    flip = jnp.where(lax.broadcasted_iota(jnp.int32, (1, depth), 1) < 2 * LEV, -1.0, 1.0)
    north_sign = jnp.where(lat == 0, flip, 1.0)
    south_sign = jnp.where(lat == n_lat - 1, flip, 1.0)
    coefs = [jnp.transpose(ref[...]) for ref in (cl_ref, ct_ref, cv_ref)]
    line_of = [g_ref[pl.ds(i, rows, stride=wide), :] for i in range(2)]
    copies = []
    for j in range(cols):
        line_of.append(g_ref[pl.ds(j + 2, rows, stride=wide), :])
        west, here, east = line_of[j : j + 3]
        first, second = first_ref[j + 1], second_ref[j + 1]
        north = north_sign * jnp.where(odd, second, first)
        south = south_sign * jnp.where(odd, first, second)
        up = jnp.where(line == 0, north, pltpu.roll(here, 1, 0))
        down = jnp.where(line == rows - 1, south, pltpu.roll(here, rows - 1, 0))
        above = jnp.where(top, 0.0, pltpu.roll(here, depth - 1, 1))
        below = jnp.where(bottom, 0.0, pltpu.roll(here, 1, 1))
        twice = 2.0 * here
        made[j] = (
            here
            + coefs[0][:, j : j + 1] * (east + west - twice)
            + coefs[1][:, j : j + 1] * (up + down - twice)
            + coefs[2][:, j : j + 1] * (above + below - twice)
        )
        if (j + 1) % size == 0:
            part = pl.ds(j + 1 - size, size)
            copies.append(pltpu.make_async_copy(made.at[part], out_ref.at[part], sems.at[j // size]))
            copies[-1].start()
    for copy in copies:
        copy.wait()


def per_device(fields, cutoff, cap_mask, coef_lon, coef_lat, coef_vert):
    rows, cols, depth = fields.shape
    peers = lax.axis_size("lon")
    n_lat = lax.axis_size("lat")
    vmem = pl.BlockSpec(memory_space=pltpu.VMEM)
    smem = pl.BlockSpec(memory_space=pltpu.SMEM)
    wide = cols + 2

    packed = pl.pallas_call(
        pack_kernel,
        out_shape=jax.ShapeDtypeStruct((rows * cols, depth), jnp.float32),
        in_specs=[pl.BlockSpec(memory_space=pl.ANY)],
        out_specs=vmem,
        scratch_shapes=[pltpu.VMEM((cols, rows, depth), jnp.float32), pltpu.SemaphoreType.DMA((6,))],
        name="pack",
    )(jnp.transpose(fields, (1, 0, 2)))
    block = lax.all_to_all(packed.reshape(peers, cols, 1, depth), "lon", 0, 0, tiled=True)
    forth, back = tables(cols * peers, cols)
    half = cols * peers // 2
    filtered = pl.pallas_call(
        functools.partial(filter_kernel, cols, peers),
        out_shape=jax.ShapeDtypeStruct((peers * wide, depth), jnp.float32),
        in_specs=[smem, smem] + [vmem] * 3,
        out_specs=vmem,
        scratch_shapes=[pltpu.VMEM((half, 2 * depth), jnp.bfloat16)] * 2,
        compiler_params=pltpu.CompilerParams(vmem_limit_bytes=24 * 1024 * 1024),
        name="filter",
    )(
        cutoff,
        cap_mask,
        block.reshape(peers * cols, depth),
        jnp.asarray(forth),
        jnp.asarray(back),
    )
    returned = lax.all_to_all(filtered.reshape(peers, wide, 1, depth), "lon", 0, 0, tiled=True)
    odd = lax.axis_index("lat") % 2 == 1
    head, tail = returned[0], returned[-1]
    first, second = [], []
    for lat in range(n_lat):
        for lon in range(peers):
            here = lat * peers + lon
            pair = lat + 1 if lat % 2 else lat - 1
            inside = 0 <= pair < n_lat
            first.append((here, pair * peers + lon if inside else lat * peers + (lon + peers // 2) % peers))
            second.append((here, (lat ^ 1) * peers + lon))
    first = lax.ppermute(jnp.where(odd, tail, head), ("lat", "lon"), first)
    second = lax.ppermute(jnp.where(odd, head, tail), ("lat", "lon"), second)
    out = pl.pallas_call(
        functools.partial(stencil_kernel, cols, rows, n_lat),
        out_shape=jax.ShapeDtypeStruct((cols, rows, depth), jnp.float32),
        in_specs=[vmem] * 6,
        out_specs=pl.BlockSpec(memory_space=pl.ANY),
        scratch_shapes=[pltpu.VMEM((cols, rows, depth), jnp.float32), pltpu.SemaphoreType.DMA((6,))],
        name="stencil",
    )(
        returned.reshape(rows * wide, depth),
        first,
        second,
        jnp.transpose(coef_lon),
        jnp.transpose(coef_lat),
        jnp.transpose(coef_vert),
    )
    return jnp.transpose(out, (1, 0, 2))


def solution(mesh):
    return jax.shard_map(
        per_device,
        mesh=mesh,
        in_specs=(
            P("lat", "lon", None),
            P(),
            P(),
            P("lat", "lon"),
            P("lat", "lon"),
            P("lat", "lon"),
        ),
        out_specs=P("lat", "lon", None),
        check_vma=False,
    )
```

```python
import functools

import jax
import jax.numpy as jnp
import ml_dtypes
import numpy as np
from jax import lax
from jax.experimental import pallas as pl
from jax.experimental.pallas import tpu as pltpu
from jax.sharding import PartitionSpec as P

LEV = 16
WAVES = 288
MIB = 1024 * 1024


def pair_table(table, width):
    high = table.astype(ml_dtypes.bfloat16)
    low = (table - high.astype(np.float64)).astype(ml_dtypes.bfloat16)
    blank = np.zeros((table.shape[0], width - 2 * table.shape[1]), ml_dtypes.bfloat16)
    return np.concatenate([high, low, blank], axis=1)


def tables(full, cols, width):
    half = full // 2
    sectors = half // cols
    place = (np.arange(cols)[:, None] + cols * np.arange(sectors)[None, :]).reshape(-1)
    made = []
    for parity in (0, 1):
        wave = np.arange(parity, WAVES, 2)
        angle = (wave[:, None] * place[None, :] % full) * (2.0 * np.pi / full)
        made.append(np.concatenate([np.cos(angle), np.sin(angle)], axis=0))
    forth = [pair_table(m, 2 * width) for m in made]
    back = np.concatenate([pair_table(m.T, width) for m in made], axis=1)
    return np.concatenate(forth + [back], axis=0)


def pack_kernel(x_ref, out_ref, held, sems):
    cols, rows, _ = x_ref.shape
    parts = sems.shape[0]
    size = cols // parts
    copies = []
    for i in range(parts):
        part = pl.ds(i * size, size)
        copies.append(pltpu.make_async_copy(x_ref.at[part], held.at[part], sems.at[i]))
        copies[-1].start()
    for i in range(parts):
        copies[i].wait()
        for j in range(i * size, (i + 1) * size):
            out_ref[pl.ds(j, rows, stride=cols), :] = held[j]


def halves(values):
    high = values.astype(jnp.bfloat16)
    low = (values - high.astype(jnp.float32)).astype(jnp.bfloat16)
    return high, low


def product(table, data):
    both = jnp.dot(table, jnp.concatenate([data, data], axis=0), preferred_element_type=jnp.float32)
    depth = both.shape[1] // 2
    return both[:, :depth] + both[:, depth:]


def filter_kernel(cols, peers, cut_ref, cap_ref, x_ref, table_ref, out_ref, even, odd):
    depth = x_ref.shape[1]
    full = cols * peers
    half = peers // 2
    wide = cols + 2
    width = table_ref.shape[1] // 2
    row = lax.axis_index("lat") * peers + lax.axis_index("lon")
    place = lax.broadcasted_iota(jnp.int32, (1, cut_ref.shape[0]), 1)
    mine = jnp.where((place == row) & (cap_ref[...].reshape(place.shape) == 1), cut_ref[...].reshape(place.shape), 0)
    cut = jnp.max(mine.astype(jnp.float32)).astype(jnp.int32)

    def emit(j, values):
        out_ref[pl.ds(1 + j, peers, stride=wide), :] = values
        if j == cols - 1:
            out_ref[pl.ds(0, peers, stride=wide), :] = pltpu.roll(values, 1, 0)
        if j == 0:
            out_ref[pl.ds(wide - 1, peers, stride=wide), :] = pltpu.roll(values, peers - 1, 0)

    @pl.when(cut == 0)
    def _():
        for j in range(cols):
            emit(j, x_ref[pl.ds(j, peers, stride=cols), :])

    @pl.when(cut != 0)
    def _():
        for j in range(cols):
            values = x_ref[pl.ds(j, peers, stride=cols), :]
            for ref, folded in ((even, values[:half] + values[half:]), (odd, values[:half] - values[half:])):
                high, low = halves(folded)
                ref[pl.ds(j * half, half), 0:depth] = high
                ref[pl.ds(j * half, half), depth : 2 * depth] = low
        back = []
        for parity, ref in ((0, even), (1, odd)):
            spectrum = product(table_ref[pl.ds(parity * WAVES, WAVES), 0 : 2 * ref.shape[0]], ref[...])
            index = lax.broadcasted_iota(jnp.int32, spectrum.shape, 0)
            count = WAVES // 2
            wave = 2 * jnp.where(index < count, index, index - count) + parity
            weight = jnp.where(wave == 0, 1.0 / full, 2.0 / full)
            spectrum = jnp.where(wave < cut, spectrum * weight, 0.0)
            table = table_ref[2 * WAVES :, pl.ds(parity * width, 2 * WAVES)]
            back.append(product(table, jnp.concatenate(halves(spectrum), axis=1)))
        for j in range(cols):
            near = back[0][j * half : (j + 1) * half]
            far = back[1][j * half : (j + 1) * half]
            emit(j, jnp.concatenate([near + far, near - far], axis=0))


def stencil_kernel(cols, rows, n_lat, g_ref, first_ref, second_ref, cl_ref, ct_ref, cv_ref, out_ref, made, sems):
    wide = cols + 2
    depth = g_ref.shape[1]
    parts = sems.shape[0]
    size = cols // parts
    lat = lax.axis_index("lat")
    odd = lat % 2 == 1
    first_edge = jnp.where((lat == 0) | (odd & (lat != n_lat - 1)), 0, 1)
    second_edge = jnp.where(odd, 1, 0)
    lane = lax.broadcasted_iota(jnp.int32, (rows, depth), 1)
    line = lax.broadcasted_iota(jnp.int32, (rows, depth), 0)
    top = lane % LEV == LEV - 1
    bottom = lane % LEV == 0
    flip = jnp.where(lax.broadcasted_iota(jnp.int32, (1, depth), 1) < 2 * LEV, -1.0, 1.0)
    north_sign = jnp.where(lat == 0, flip, 1.0)
    south_sign = jnp.where(lat == n_lat - 1, flip, 1.0)
    coefs = [jnp.transpose(ref[...]) for ref in (cl_ref, ct_ref, cv_ref)]
    line_of = [g_ref[pl.ds(i, rows, stride=wide), :] for i in range(2)]
    copies = []
    for j in range(cols):
        line_of.append(g_ref[pl.ds(j + 2, rows, stride=wide), :])
        west, here, east = line_of[j : j + 3]
        first, second = first_ref[first_edge, j + 1], second_ref[second_edge, j + 1]
        north = north_sign * jnp.where(odd, second, first)
        south = south_sign * jnp.where(odd, first, second)
        up = jnp.where(line == 0, north, pltpu.roll(here, 1, 0))
        down = jnp.where(line == rows - 1, south, pltpu.roll(here, rows - 1, 0))
        above = jnp.where(top, 0.0, pltpu.roll(here, depth - 1, 1))
        below = jnp.where(bottom, 0.0, pltpu.roll(here, 1, 1))
        twice = 2.0 * here
        made[j] = (
            here
            + coefs[0][:, j : j + 1] * (east + west - twice)
            + coefs[1][:, j : j + 1] * (up + down - twice)
            + coefs[2][:, j : j + 1] * (above + below - twice)
        )
        if (j + 1) % size == 0:
            part = pl.ds(j + 1 - size, size)
            copies.append(pltpu.make_async_copy(made.at[part], out_ref.at[part], sems.at[j // size]))
            copies[-1].start()
    for copy in copies:
        copy.wait()


def per_device(fields, cutoff, cap_mask, coef_lon, coef_lat, coef_vert):
    rows, cols, depth = fields.shape
    peers = lax.axis_size("lon")
    n_lat = lax.axis_size("lat")
    vmem = pl.BlockSpec(memory_space=pltpu.VMEM)
    wide = cols + 2

    packed = pl.pallas_call(
        pack_kernel,
        out_shape=pltpu.VMEM((rows * cols, depth), jnp.float32),
        in_specs=[pl.BlockSpec(memory_space=pltpu.HBM)],
        out_specs=vmem,
        scratch_shapes=[pltpu.VMEM((cols, rows, depth), jnp.float32), pltpu.SemaphoreType.DMA((6,))],
        compiler_params=pltpu.CompilerParams(vmem_limit_bytes=4 * MIB),
        cost_estimate=pl.CostEstimate(flops=10000000000, bytes_accessed=67108864, transcendentals=0),
        name="pack",
    )(pltpu.with_memory_space_constraint(jnp.transpose(fields, (1, 0, 2)), pltpu.HBM))
    block = lax.all_to_all(packed.reshape(peers, cols, 1, depth), "lon", 0, 0, tiled=True)
    table = tables(cols * peers, cols, 640)
    half = cols * peers // 2
    filtered = pl.pallas_call(
        functools.partial(filter_kernel, cols, peers),
        out_shape=jax.ShapeDtypeStruct((peers * wide, depth), jnp.float32),
        in_specs=[vmem] * 4,
        out_specs=vmem,
        scratch_shapes=[pltpu.VMEM((half, 2 * depth), jnp.bfloat16)] * 2,
        compiler_params=pltpu.CompilerParams(vmem_limit_bytes=16 * MIB),
        name="filter",
    )(
        cutoff,
        cap_mask,
        block.reshape(peers * cols, depth),
        jnp.asarray(table),
    )
    returned = lax.all_to_all(filtered.reshape(peers, wide, 1, depth), "lon", 0, 0, tiled=True)
    edges = jnp.stack([returned[0], returned[-1]])
    first, second = [], []
    for lat in range(n_lat):
        for lon in range(peers):
            here = lat * peers + lon
            pair = lat + 1 if lat % 2 else lat - 1
            inside = 0 <= pair < n_lat
            first.append((here, pair * peers + lon if inside else lat * peers + (lon + peers // 2) % peers))
            second.append((here, (lat ^ 1) * peers + lon))
    first = lax.ppermute(edges, ("lat", "lon"), first)
    second = lax.ppermute(edges, ("lat", "lon"), second)
    out = pl.pallas_call(
        functools.partial(stencil_kernel, cols, rows, n_lat),
        out_shape=jax.ShapeDtypeStruct((cols, rows, depth), jnp.float32),
        in_specs=[vmem] * 6,
        out_specs=pl.BlockSpec(memory_space=pl.ANY),
        scratch_shapes=[pltpu.VMEM((cols, rows, depth), jnp.float32), pltpu.SemaphoreType.DMA((6,))],
        compiler_params=pltpu.CompilerParams(vmem_limit_bytes=8 * MIB),
        name="stencil",
    )(
        returned.reshape(rows * wide, depth),
        first,
        second,
        jnp.transpose(coef_lon),
        jnp.transpose(coef_lat),
        jnp.transpose(coef_vert),
    )
    return jnp.transpose(out, (1, 0, 2))


def solution(mesh):
    return jax.shard_map(
        per_device,
        mesh=mesh,
        in_specs=(
            P("lat", "lon", None),
            P(),
            P(),
            P("lat", "lon"),
            P("lat", "lon"),
            P("lat", "lon"),
        ),
        out_specs=P("lat", "lon", None),
        check_vma=False,
    )
```

```python
import functools

import jax
import jax.numpy as jnp
import ml_dtypes
import numpy as np
from jax import lax
from jax.experimental import pallas as pl
from jax.experimental.pallas import tpu as pltpu
from jax.sharding import PartitionSpec as P

LEV = 16
WAVES = 288
STEPS = 3
MIB = 1024 * 1024
TILE = 8


def pair_table(table, width):
    high = table.astype(ml_dtypes.bfloat16)
    low = (table - high.astype(np.float64)).astype(ml_dtypes.bfloat16)
    blank = np.zeros((table.shape[0], width - 2 * table.shape[1]), ml_dtypes.bfloat16)
    return np.concatenate([high, low, blank], axis=1)


def tables(full, cols, width):
    half = full // 2
    sectors = half // cols
    place = (np.arange(cols)[:, None] + cols * np.arange(sectors)[None, :]).reshape(-1)
    made = []
    for parity in (0, 1):
        wave = np.arange(parity, WAVES, 2)
        angle = (wave[:, None] * place[None, :] % full) * (2.0 * np.pi / full)
        made.append(np.concatenate([np.cos(angle), np.sin(angle)], axis=0))
    forth = [pair_table(m, 2 * width) for m in made]
    back = np.concatenate([pair_table(m.T, width) for m in made], axis=1)
    return np.concatenate(forth + [back], axis=0)


def pack_kernel(x_ref, out_ref, odd_ref, even_ref, held, sems):
    odd = lax.axis_index("lat") % 2 == 1
    odd_ref[...] = jnp.full(odd_ref.shape, jnp.where(odd, 1.0, 0.0), jnp.float32)
    even_ref[...] = jnp.full(even_ref.shape, jnp.where(odd, 0.0, 1.0), jnp.float32)
    cols, rows, _ = x_ref.shape
    parts = sems.shape[0]
    size = cols // parts
    copies = []
    for i in range(parts):
        part = pl.ds(i * size, size)
        copies.append(pltpu.make_async_copy(x_ref.at[part], held.at[part], sems.at[i]))
        copies[-1].start()
    for i in range(parts):
        copies[i].wait()
        for j in range(i * size, (i + 1) * size):
            out_ref[pl.ds(j, rows, stride=cols), :] = held[j]


def halves(values):
    high = values.astype(jnp.bfloat16)
    low = (values - high.astype(jnp.float32)).astype(jnp.bfloat16)
    return high, low


def product(table, data):
    both = jnp.dot(table, jnp.concatenate([data, data], axis=0), preferred_element_type=jnp.float32)
    depth = both.shape[1] // 2
    return both[:, :depth] + both[:, depth:]


def filter_kernel(cols, peers, cut_ref, cap_ref, x_ref, table_ref, out_ref, even, odd):
    depth = x_ref.shape[1]
    full = cols * peers
    half = peers // 2
    wide = cols + 2
    width = table_ref.shape[1] // 2
    row = lax.axis_index("lat") * peers + lax.axis_index("lon")
    place = lax.broadcasted_iota(jnp.int32, (1, cut_ref.shape[0]), 1)
    mine = jnp.where((place == row) & (cap_ref[...].reshape(place.shape) == 1), cut_ref[...].reshape(place.shape), 0)
    cut = jnp.max(mine.astype(jnp.float32)).astype(jnp.int32)

    def emit(j, values):
        out_ref[pl.ds(1 + j, peers, stride=wide), :] = values
        if j == cols - 1:
            out_ref[pl.ds(0, peers, stride=wide), :] = pltpu.roll(values, 1, 0)
        if j == 0:
            out_ref[pl.ds(wide - 1, peers, stride=wide), :] = pltpu.roll(values, peers - 1, 0)

    @pl.when(cut == 0)
    def _():
        for j in range(cols):
            emit(j, x_ref[pl.ds(j, peers, stride=cols), :])

    @pl.when(cut != 0)
    def _():
        for j in range(cols):
            values = x_ref[pl.ds(j, peers, stride=cols), :]
            for ref, folded in ((even, values[:half] + values[half:]), (odd, values[:half] - values[half:])):
                high, low = halves(folded)
                ref[pl.ds(j * half, half), 0:depth] = high
                ref[pl.ds(j * half, half), depth : 2 * depth] = low
        spectra = []
        for parity, ref in ((0, even), (1, odd)):
            spectrum = product(table_ref[pl.ds(parity * WAVES, WAVES), 0 : 2 * ref.shape[0]], ref[...])
            index = lax.broadcasted_iota(jnp.int32, spectrum.shape, 0)
            count = WAVES // 2
            wave = 2 * jnp.where(index < count, index, index - count) + parity
            weight = jnp.where(wave == 0, 1.0 / full, 2.0 / full)
            spectrum = jnp.where(wave < cut, spectrum * weight, 0.0)
            spectra.append(jnp.concatenate(halves(spectrum), axis=1))
        step = cols // STEPS
        for i in range(STEPS):
            part = pl.ds(2 * WAVES + i * step * half, step * half)
            back = [
                product(table_ref[part, parity * width : parity * width + 2 * WAVES], spectra[parity]) for parity in (0, 1)
            ]
            for j in range(step):
                near = back[0][j * half : (j + 1) * half]
                far = back[1][j * half : (j + 1) * half]
                emit(i * step + j, jnp.concatenate([near + far, near - far], axis=0))


def stencil_kernel(cols, rows, n_lat, g_ref, cl_ref, ct_ref, cv_ref, out_ref, rim_ref, share_ref, made, sems):
    wide = cols + 2
    depth = g_ref.shape[1]
    parts = sems.shape[0]
    size = cols // parts
    lat = lax.axis_index("lat")
    inner = pl.ds(TILE, rows - 2 * TILE)
    lane = lax.broadcasted_iota(jnp.int32, (rows, depth), 1)
    line = lax.broadcasted_iota(jnp.int32, (rows, depth), 0)
    top = lane % LEV == LEV - 1
    bottom = lane % LEV == 0
    flip = jnp.where(lax.broadcasted_iota(jnp.int32, (1, depth), 1) < 2 * LEV, -1.0, 1.0)
    north_sign = jnp.where(lat == 0, flip, 1.0)
    south_sign = jnp.where(lat == n_lat - 1, flip, 1.0)
    coefs = [jnp.transpose(ref[...]) for ref in (cl_ref, ct_ref, cv_ref)]
    line_of = [g_ref[pl.ds(i, rows, stride=wide), :] for i in range(2)]
    copies = []
    for j in range(cols):
        line_of.append(g_ref[pl.ds(j + 2, rows, stride=wide), :])
        west, here, east = line_of[j : j + 3]
        up = jnp.where(line == 0, 0.0, pltpu.roll(here, 1, 0))
        down = jnp.where(line == rows - 1, 0.0, pltpu.roll(here, rows - 1, 0))
        above = jnp.where(top, 0.0, pltpu.roll(here, depth - 1, 1))
        below = jnp.where(bottom, 0.0, pltpu.roll(here, 1, 1))
        twice = 2.0 * here
        lat_share = coefs[1][:, j : j + 1]
        value = (
            here
            + coefs[0][:, j : j + 1] * (east + west - twice)
            + lat_share * (up + down - twice)
            + coefs[2][:, j : j + 1] * (above + below - twice)
        )
        made[j] = value
        rim_ref[0, j] = value[:TILE]
        rim_ref[1, j] = value[rows - TILE :]
        share_ref[0, j] = lat_share[:1] * north_sign
        share_ref[1, j] = lat_share[rows - 1 :] * south_sign
        if (j + 1) % size == 0:
            part = pl.ds(j + 1 - size, size)
            copies.append(pltpu.make_async_copy(made.at[part, inner], out_ref.at[part, inner], sems.at[j // size]))
            copies[-1].start()
    for copy in copies:
        copy.wait()


def rim_kernel(cols, _, rim_ref, share_ref, first_ref, second_ref, out_ref, made, sems):
    rows = out_ref.shape[1]
    odd = lax.axis_index("lat") % 2 == 1
    line = lax.broadcasted_iota(jnp.int32, rim_ref.shape[2:], 0)
    for j in range(cols):
        first, second = first_ref[j], second_ref[j]
        north = share_ref[0, j] * jnp.where(odd, second, first)
        south = share_ref[1, j] * jnp.where(odd, first, second)
        made[0, j] = rim_ref[0, j] + jnp.where(line == 0, north, 0.0)
        made[1, j] = rim_ref[1, j] + jnp.where(line == TILE - 1, south, 0.0)
    copies = [
        pltpu.make_async_copy(made.at[edge], out_ref.at[:, pl.ds(edge * (rows - TILE), TILE)], sems.at[edge])
        for edge in (0, 1)
    ]
    for copy in copies:
        copy.start()
    for copy in copies:
        copy.wait()


def per_device(fields, cutoff, cap_mask, coef_lon, coef_lat, coef_vert):
    rows, cols, depth = fields.shape
    peers = lax.axis_size("lon")
    n_lat = lax.axis_size("lat")
    vmem = pl.BlockSpec(memory_space=pltpu.VMEM)
    hbm = pl.BlockSpec(memory_space=pltpu.HBM)
    wide = cols + 2

    packed, odd, even = pl.pallas_call(
        pack_kernel,
        out_shape=(
            pltpu.VMEM((rows * cols, depth), jnp.float32),
            pltpu.VMEM((1, 1, depth), jnp.float32),
            pltpu.VMEM((1, 1, depth), jnp.float32),
        ),
        in_specs=[pl.BlockSpec(memory_space=pltpu.HBM)],
        out_specs=(vmem, vmem, vmem),
        scratch_shapes=[pltpu.VMEM((cols, rows, depth), jnp.float32), pltpu.SemaphoreType.DMA((6,))],
        compiler_params=pltpu.CompilerParams(vmem_limit_bytes=4 * MIB),
        cost_estimate=pl.CostEstimate(flops=10000000000, bytes_accessed=67108864, transcendentals=0),
        name="pack",
    )(pltpu.with_memory_space_constraint(jnp.transpose(fields, (1, 0, 2)), pltpu.HBM))
    block = lax.all_to_all(packed.reshape(peers, cols, 1, depth), "lon", 0, 0, tiled=True)
    table = tables(cols * peers, cols, 640)
    half = cols * peers // 2
    filtered = pl.pallas_call(
        functools.partial(filter_kernel, cols, peers),
        out_shape=jax.ShapeDtypeStruct((peers * wide, depth), jnp.float32),
        in_specs=[vmem] * 4,
        out_specs=vmem,
        scratch_shapes=[pltpu.VMEM((half, 2 * depth), jnp.bfloat16)] * 2,
        compiler_params=pltpu.CompilerParams(vmem_limit_bytes=16 * MIB),
        name="filter",
    )(
        cutoff,
        cap_mask,
        block.reshape(peers * cols, depth),
        jnp.asarray(table),
    )
    returned = lax.all_to_all(filtered.reshape(peers, wide, 1, depth), "lon", 0, 0, tiled=True)
    head, tail = returned[0, 1:-1], returned[-1, 1:-1]
    edges = jnp.stack([returned[0], returned[-1]])
    first, second = [], []
    for lat in range(n_lat):
        for lon in range(peers):
            here = lat * peers + lon
            pair = lat + 1 if lat % 2 else lat - 1
            inside = 0 <= pair < n_lat
            first.append((here, pair * peers + lon if inside else lat * peers + (lon + peers // 2) % peers))
            second.append((here, (lat ^ 1) * peers + lon))
    first = lax.ppermute(odd * tail + even * head, ("lat", "lon"), first)
    second = lax.ppermute(odd * head + even * tail, ("lat", "lon"), second)
    rim_shape = (2, cols, TILE, depth)
    out, rim, share = pl.pallas_call(
        functools.partial(stencil_kernel, cols, rows, n_lat),
        out_shape=(
            pltpu.HBM((cols, rows, depth), jnp.float32),
            pltpu.VMEM(rim_shape, jnp.float32),
            pltpu.VMEM((2, cols, 1, depth), jnp.float32),
        ),
        in_specs=[vmem] * 4,
        out_specs=(hbm, vmem, vmem),
        scratch_shapes=[pltpu.VMEM((cols, rows, depth), jnp.float32), pltpu.SemaphoreType.DMA((6,))],
        compiler_params=pltpu.CompilerParams(vmem_limit_bytes=8 * MIB),
        cost_estimate=pl.CostEstimate(flops=10**9, bytes_accessed=2 * MIB, transcendentals=0),
        name="stencil",
    )(returned.reshape(rows * wide, depth), jnp.transpose(coef_lon), jnp.transpose(coef_lat), jnp.transpose(coef_vert))
    out = pl.pallas_call(
        functools.partial(rim_kernel, cols),
        out_shape=jax.ShapeDtypeStruct((cols, rows, depth), jnp.float32),
        in_specs=[hbm] + [vmem] * 4,
        out_specs=hbm,
        scratch_shapes=[pltpu.VMEM(rim_shape, jnp.float32), pltpu.SemaphoreType.DMA((2,))],
        input_output_aliases={0: 0},
        compiler_params=pltpu.CompilerParams(vmem_limit_bytes=4 * MIB),
        name="rim",
    )(out, rim, share, first, second)
    return jnp.transpose(out, (1, 0, 2))


def solution(mesh):
    return jax.shard_map(
        per_device,
        mesh=mesh,
        in_specs=(
            P("lat", "lon", None),
            P(),
            P(),
            P("lat", "lon"),
            P("lat", "lon"),
            P("lat", "lon"),
        ),
        out_specs=P("lat", "lon", None),
        check_vma=False,
    )
```

```python
import functools

import jax
import jax.numpy as jnp
import ml_dtypes
import numpy as np
from jax import lax
from jax.experimental import pallas as pl
from jax.experimental.pallas import tpu as pltpu
from jax.sharding import PartitionSpec as P

LEV = 16
WAVES = 288
BACK_WIDTH = 384
STEPS = 1
MIB = 1024 * 1024
TILE = 8
LATE = 12


def pair_table(table, width):
    high = table.astype(ml_dtypes.bfloat16)
    low = (table - high.astype(np.float64)).astype(ml_dtypes.bfloat16)
    blank = np.zeros((table.shape[0], width - 2 * table.shape[1]), ml_dtypes.bfloat16)
    return np.concatenate([high, low, blank], axis=1)


def ring(peers):
    count = peers // 4
    return [q * count + (count - 1 - i if q % 2 else i) for q in range(4) for i in range(count)]


def pairs(cols):
    return [j for i in range(cols // 2) for j in (i, cols - 1 - i)]


def tables(full, cols):
    sectors = full // cols // 4
    forth, back = [], []
    for parity in (0, 1):
        for curve in (np.cos, np.sin):
            for made, columns in ((forth, np.arange(cols)), (back, np.array(pairs(cols)))):
                place = (columns[:, None] + cols * np.arange(sectors)[None, :]).reshape(-1)
                wave = np.arange(parity, WAVES, 2)
                made.append(curve(wave[:, None] * (2 * place[None, :] + 1) % (2 * full) * (np.pi / full)))
    width = 2 * BACK_WIDTH
    below = [np.concatenate([pair_table(m.T, BACK_WIDTH) for m in back[i : i + 2]], axis=1) for i in (0, 2)]
    return np.concatenate([pair_table(m, width) for m in forth] + below, axis=0)


def pack_kernel(x_ref, out_ref, odd_ref, even_ref, held, sems):
    odd = lax.axis_index("lat") % 2 == 1
    odd_ref[...] = jnp.full(odd_ref.shape, jnp.where(odd, 1.0, 0.0), jnp.float32)
    even_ref[...] = jnp.full(even_ref.shape, jnp.where(odd, 0.0, 1.0), jnp.float32)
    cols, rows, _ = x_ref.shape
    parts = sems.shape[0]
    size = cols // parts
    copies = []
    for i in range(parts):
        part = pl.ds(i * size, size)
        copies.append(pltpu.make_async_copy(x_ref.at[part], held.at[part], sems.at[i]))
        copies[-1].start()
    for i in range(parts):
        copies[i].wait()
        for j in range(i * size, (i + 1) * size):
            out_ref[pl.ds(j, rows, stride=cols), :] = held[j]


def halves(values):
    high = values.astype(jnp.bfloat16)
    low = (values - high.astype(jnp.float32)).astype(jnp.bfloat16)
    return high, low


def product(table, data):
    both = jnp.dot(table, jnp.concatenate([data, data], axis=0), preferred_element_type=jnp.float32)
    depth = both.shape[1] // 2
    return both[:, :depth] + both[:, depth:]


def filter_kernel(cols, peers, cut_ref, cap_ref, x_ref, table_ref, out_ref, folds):
    depth = x_ref.shape[1]
    full = cols * peers
    count = peers // 4
    wide = cols + 2
    waves = WAVES // 2
    quarter = cols * count
    sector = lax.axis_index("lon")
    turn = sector // count
    place = jnp.where(turn % 2 == 1, (2 * turn + 1) * count - 1 - sector, sector)
    row = lax.axis_index("lat") * peers + place
    line = lax.broadcasted_iota(jnp.int32, (1, cut_ref.shape[0]), 1)
    mine = jnp.where((line == row) & (cap_ref[...].reshape(line.shape) == 1), cut_ref[...].reshape(line.shape), 0)
    cut = jnp.max(mine.astype(jnp.float32)).astype(jnp.int32)
    index = lax.broadcasted_iota(jnp.int32, (count, depth), 0)

    def lower(block, first):
        return jnp.where(index == 0, first, pltpu.roll(block, 1, 0))

    def upper(block, last):
        return jnp.where(index == count - 1, last, pltpu.roll(block, count - 1, 0))

    def emit(j, blocks):
        a, b, c, d = blocks
        rows = [(1 + j, blocks)]
        if j == cols - 1:
            rows.append((0, (lower(a, d[:1]), upper(b, a[-1:]), lower(c, b[:1]), upper(d, c[-1:]))))
        if j == 0:
            rows.append((wide - 1, (upper(a, b[-1:]), lower(b, c[:1]), upper(c, d[-1:]), lower(d, a[:1]))))
        for i, values in rows:
            out_ref[pl.ds(i, peers, stride=wide), :] = jnp.concatenate(values, axis=0)

    def column(j):
        return [x_ref[pl.ds(q * quarter + j, count, stride=cols), :] for q in range(4)]

    @pl.when(cut == 0)
    def _():
        for j in range(cols):
            emit(j, column(j))

    @pl.when(cut != 0)
    def _():
        for j in range(cols):
            a, _, c, _ = column(j)
            _, b, _, d = column(cols - 1 - j)
            for parity, (here, mirror) in enumerate(((a + c, d + b), (a - c, d - b))):
                for kind, folded in enumerate((here + mirror, here - mirror)):
                    high, low = halves(folded)
                    part = pl.ds(j * count, count)
                    folds[2 * parity + kind, part, 0:depth] = high
                    folds[2 * parity + kind, part, depth : 2 * depth] = low
        spectra = []
        for i in range(4):
            spectrum = product(table_ref[pl.ds(i * waves, waves), 0 : 2 * quarter], folds[i])
            wave = 2 * lax.broadcasted_iota(jnp.int32, spectrum.shape, 0) + i // 2
            weight = jnp.where(wave == 0, 1.0 / full, 2.0 / full)
            spectrum = jnp.where(wave < cut, spectrum * weight, 0.0)
            spectra.append(jnp.concatenate(halves(spectrum), axis=1))
        step = cols // STEPS
        order = pairs(cols)
        for k in range(STEPS):
            parts = []
            for i in range(4):
                part = pl.ds(4 * waves + i // 2 * quarter + k * step * count, step * count)
                start = i % 2 * BACK_WIDTH
                parts.append(product(table_ref[part, start : start + 2 * waves], spectra[i]))
            made = {}
            for t in range(step):
                ce, se, co, so = [p[t * count : (t + 1) * count] for p in parts]
                j = order[k * step + t]
                made[j, 0], made[cols - 1 - j, 3] = (ce + co) + (se + so), (ce + co) - (se + so)
                made[j, 2], made[cols - 1 - j, 1] = (ce - co) + (se - so), (ce - co) - (se - so)
                if t % 2 == 1:
                    for i in (order[k * step + t - 1], j):
                        emit(i, [made[i, q] for q in range(4)])


def stencil_kernel(cols, rows, n_lat, g_ref, cl_ref, ct_ref, cv_ref, out_ref, rim_ref, share_ref, late_ref, made, sems):
    wide = cols + 2
    depth = g_ref.shape[1]
    early = made.shape[0]
    size = early // sems.shape[0]
    lat = lax.axis_index("lat")
    inner = pl.ds(TILE, rows - 2 * TILE)
    lane = lax.broadcasted_iota(jnp.int32, (rows, depth), 1)
    line = lax.broadcasted_iota(jnp.int32, (rows, depth), 0)
    top = lane % LEV == LEV - 1
    bottom = lane % LEV == 0
    flip = jnp.where(lax.broadcasted_iota(jnp.int32, (1, depth), 1) < 2 * LEV, -1.0, 1.0)
    north_sign = jnp.where(lat == 0, flip, 1.0)
    south_sign = jnp.where(lat == n_lat - 1, flip, 1.0)
    coefs = [jnp.transpose(ref[...]) for ref in (cl_ref, ct_ref, cv_ref)]
    line_of = [g_ref[pl.ds(i, rows, stride=wide), :] for i in range(2)]
    copies = []
    for j in range(cols):
        line_of.append(g_ref[pl.ds(j + 2, rows, stride=wide), :])
        west, here, east = line_of[j : j + 3]
        up = jnp.where(line == 0, 0.0, pltpu.roll(here, 1, 0))
        down = jnp.where(line == rows - 1, 0.0, pltpu.roll(here, rows - 1, 0))
        above = jnp.where(top, 0.0, pltpu.roll(here, depth - 1, 1))
        below = jnp.where(bottom, 0.0, pltpu.roll(here, 1, 1))
        twice = 2.0 * here
        lat_share = coefs[1][:, j : j + 1]
        value = (
            here
            + coefs[0][:, j : j + 1] * (east + west - twice)
            + lat_share * (up + down - twice)
            + coefs[2][:, j : j + 1] * (above + below - twice)
        )
        if j < early:
            made[j] = value[TILE : rows - TILE]
        else:
            late_ref[j - early] = value[TILE : rows - TILE]
        rim_ref[0, j] = value[:TILE]
        rim_ref[1, j] = value[rows - TILE :]
        share_ref[0, j] = lat_share[:1] * north_sign
        share_ref[1, j] = lat_share[rows - 1 :] * south_sign
        if j < early and (j + 1) % size == 0:
            part = pl.ds(j + 1 - size, size)
            copies.append(pltpu.make_async_copy(made.at[part], out_ref.at[part, inner], sems.at[j // size]))
            copies[-1].start()
    for copy in copies:
        copy.wait()


def rim_kernel(cols, _, rim_ref, share_ref, late_ref, first_ref, second_ref, out_ref, made, sems):
    rows = out_ref.shape[1]
    late = pl.ds(cols - late_ref.shape[0], late_ref.shape[0])
    copies = [pltpu.make_async_copy(late_ref, out_ref.at[late, pl.ds(TILE, rows - 2 * TILE)], sems.at[2])]
    copies[0].start()
    odd = lax.axis_index("lat") % 2 == 1
    line = lax.broadcasted_iota(jnp.int32, rim_ref.shape[2:], 0)
    for j in range(cols):
        first, second = first_ref[j], second_ref[j]
        north = share_ref[0, j] * jnp.where(odd, second, first)
        south = share_ref[1, j] * jnp.where(odd, first, second)
        made[0, j] = rim_ref[0, j] + jnp.where(line == 0, north, 0.0)
        made[1, j] = rim_ref[1, j] + jnp.where(line == TILE - 1, south, 0.0)
    for edge in (0, 1):
        there = out_ref.at[:, pl.ds(edge * (rows - TILE), TILE)]
        copies.append(pltpu.make_async_copy(made.at[edge], there, sems.at[edge]))
        copies[-1].start()
    for copy in copies:
        copy.wait()


def per_device(fields, cutoff, cap_mask, coef_lon, coef_lat, coef_vert):
    rows, cols, depth = fields.shape
    peers = lax.axis_size("lon")
    n_lat = lax.axis_size("lat")
    vmem = pl.BlockSpec(memory_space=pltpu.VMEM)
    hbm = pl.BlockSpec(memory_space=pltpu.HBM)
    wide = cols + 2

    packed, odd, even = pl.pallas_call(
        pack_kernel,
        out_shape=(
            pltpu.VMEM((rows * cols, depth), jnp.float32),
            pltpu.VMEM((1, 1, depth), jnp.float32),
            pltpu.VMEM((1, 1, depth), jnp.float32),
        ),
        in_specs=[pl.BlockSpec(memory_space=pltpu.HBM)],
        out_specs=(vmem, vmem, vmem),
        scratch_shapes=[pltpu.VMEM((cols, rows, depth), jnp.float32), pltpu.SemaphoreType.DMA((2,))],
        compiler_params=pltpu.CompilerParams(vmem_limit_bytes=4 * MIB),
        cost_estimate=pl.CostEstimate(flops=10000000000, bytes_accessed=67108864, transcendentals=0),
        name="pack",
    )(pltpu.with_memory_space_constraint(jnp.transpose(fields, (1, 0, 2)), pltpu.HBM))
    order = [ring(peers)]
    block = lax.all_to_all(packed.reshape(peers, cols, 1, depth), "lon", 0, 0, axis_index_groups=order, tiled=True)
    table = tables(cols * peers, cols)
    filtered = pl.pallas_call(
        functools.partial(filter_kernel, cols, peers),
        out_shape=jax.ShapeDtypeStruct((peers * wide, depth), jnp.float32),
        in_specs=[vmem] * 4,
        out_specs=vmem,
        scratch_shapes=[pltpu.VMEM((4, cols * peers // 4, 2 * depth), jnp.bfloat16)],
        compiler_params=pltpu.CompilerParams(vmem_limit_bytes=16 * MIB),
        name="filter",
    )(
        cutoff,
        cap_mask,
        block.reshape(peers * cols, depth),
        jnp.asarray(table),
    )
    returned = lax.all_to_all(
        filtered.reshape(peers, wide, 1, depth), "lon", 0, 0, axis_index_groups=order, tiled=True
    )
    head, tail = returned[0, 1:-1], returned[-1, 1:-1]
    first, second = [], []
    for lat in range(n_lat):
        for lon in range(peers):
            here = lat * peers + lon
            pair = lat + 1 if lat % 2 else lat - 1
            inside = 0 <= pair < n_lat
            first.append((here, pair * peers + lon if inside else lat * peers + (lon + peers // 2) % peers))
            second.append((here, (lat ^ 1) * peers + lon))
    first = lax.ppermute(odd * tail + even * head, ("lat", "lon"), first)
    second = lax.ppermute(odd * head + even * tail, ("lat", "lon"), second)
    rim_shape = (2, cols, TILE, depth)
    out, rim, share, late = pl.pallas_call(
        functools.partial(stencil_kernel, cols, rows, n_lat),
        out_shape=(
            pltpu.HBM((cols, rows, depth), jnp.float32),
            pltpu.VMEM(rim_shape, jnp.float32),
            pltpu.VMEM((2, cols, 1, depth), jnp.float32),
            pltpu.VMEM((LATE, rows - 2 * TILE, depth), jnp.float32),
        ),
        in_specs=[vmem] * 4,
        out_specs=(hbm, vmem, vmem, vmem),
        scratch_shapes=[
            pltpu.VMEM((cols - LATE, rows - 2 * TILE, depth), jnp.float32),
            pltpu.SemaphoreType.DMA((3,)),
        ],
        compiler_params=pltpu.CompilerParams(vmem_limit_bytes=8 * MIB),
        cost_estimate=pl.CostEstimate(flops=10**9, bytes_accessed=2 * MIB, transcendentals=0),
        name="stencil",
    )(returned.reshape(rows * wide, depth), jnp.transpose(coef_lon), jnp.transpose(coef_lat), jnp.transpose(coef_vert))
    out = pl.pallas_call(
        functools.partial(rim_kernel, cols),
        out_shape=jax.ShapeDtypeStruct((cols, rows, depth), jnp.float32),
        in_specs=[hbm] + [vmem] * 5,
        out_specs=hbm,
        scratch_shapes=[pltpu.VMEM(rim_shape, jnp.float32), pltpu.SemaphoreType.DMA((3,))],
        input_output_aliases={0: 0},
        compiler_params=pltpu.CompilerParams(vmem_limit_bytes=4 * MIB),
        name="rim",
    )(out, rim, share, late, first, second)
    return jnp.transpose(out, (1, 0, 2))


def solution(mesh):
    return jax.shard_map(
        per_device,
        mesh=mesh,
        in_specs=(
            P("lat", "lon", None),
            P(),
            P(),
            P("lat", "lon"),
            P("lat", "lon"),
            P("lat", "lon"),
        ),
        out_specs=P("lat", "lon", None),
        check_vma=False,
    )
```

```python
import functools

import jax
import jax.numpy as jnp
import ml_dtypes
import numpy as np
from jax import lax
from jax.experimental import pallas as pl
from jax.experimental.pallas import tpu as pltpu
from jax.sharding import PartitionSpec as P

LEV = 16
WAVES = 288
BACK_WIDTH = 384
FIRST = 13
STEPS = 1
MIB = 1024 * 1024
TILE = 8
LATE = 12


def pair_table(table, width):
    high = table.astype(ml_dtypes.bfloat16)
    low = (table - high.astype(np.float64)).astype(ml_dtypes.bfloat16)
    blank = np.zeros((table.shape[0], width - 2 * table.shape[1]), ml_dtypes.bfloat16)
    return np.concatenate([high, low, blank], axis=1)


def ring(peers):
    count = peers // 4
    return [-q % 4 * count + (FIRST - i) % count for q in range(4) for i in range(count)]


def pairs(cols):
    return [j for i in range(cols // 2) for j in (i, cols - 1 - i)]


def tables(full, cols):
    sectors = np.array(ring(full // cols)[: full // cols // 4])
    forth, back = [], []
    for parity in (0, 1):
        for curve in (np.cos, np.sin):
            for made, columns in ((forth, np.arange(cols)), (back, np.array(pairs(cols)))):
                place = (columns[:, None] + cols * sectors[None, :]).reshape(-1)
                wave = np.arange(parity, WAVES, 2)
                made.append(curve(wave[:, None] * (2 * place[None, :] + 1) % (2 * full) * (np.pi / full)))
    width = 2 * BACK_WIDTH
    below = [np.concatenate([pair_table(m.T, BACK_WIDTH) for m in back[i : i + 2]], axis=1) for i in (0, 2)]
    return np.concatenate([pair_table(m, width) for m in forth] + below, axis=0)


def pack_kernel(x_ref, out_ref, odd_ref, even_ref, held, sems):
    odd = lax.axis_index("lat") % 2 == 1
    odd_ref[...] = jnp.full(odd_ref.shape, jnp.where(odd, 1.0, 0.0), jnp.float32)
    even_ref[...] = jnp.full(even_ref.shape, jnp.where(odd, 0.0, 1.0), jnp.float32)
    cols, rows, _ = x_ref.shape
    parts = sems.shape[0]
    size = cols // parts
    copies = []
    for i in range(parts):
        part = pl.ds(i * size, size)
        copies.append(pltpu.make_async_copy(x_ref.at[part], held.at[part], sems.at[i]))
        copies[-1].start()
    for i in range(parts):
        copies[i].wait()
        for j in range(i * size, (i + 1) * size):
            out_ref[pl.ds(j, rows, stride=cols), :] = held[j]


def halves(values):
    high = values.astype(jnp.bfloat16)
    low = (values - high.astype(jnp.float32)).astype(jnp.bfloat16)
    return high, low


def product(table, data):
    both = jnp.dot(table, jnp.concatenate([data, data], axis=0), preferred_element_type=jnp.float32)
    depth = both.shape[1] // 2
    return both[:, :depth] + both[:, depth:]


def filter_kernel(cols, peers, cut_ref, cap_ref, x_ref, table_ref, out_ref, folds, turned, made_turned):
    depth = x_ref.shape[1]
    full = cols * peers
    count = peers // 4
    wide = cols + 2
    waves = WAVES // 2
    quarter = cols * count
    sector = lax.axis_index("lon")
    turn = (4 - sector // count) % 4
    row = lax.axis_index("lat") * peers + turn * count + (FIRST + count - sector % count) % count
    line = lax.broadcasted_iota(jnp.int32, (1, cut_ref.shape[0]), 1)
    mine = jnp.where((line == row) & (cap_ref[...].reshape(line.shape) == 1), cut_ref[...].reshape(line.shape), 0)
    cut = jnp.max(mine.astype(jnp.float32)).astype(jnp.int32)
    index = lax.broadcasted_iota(jnp.int32, (count, depth), 0)

    last = {False: (FIRST + 1) % count, True: FIRST}
    first = {False: FIRST, True: (FIRST + 1) % count}

    def before(blocks, x, kinds):
        other = (x - 1) % 4
        edge = last[kinds[other]]
        rolled = pltpu.roll(blocks[x], 1 if kinds[x] else count - 1, 0)
        return jnp.where(index == first[kinds[x]], blocks[other][edge : edge + 1], rolled)

    def after(blocks, x, kinds):
        other = (x + 1) % 4
        edge = first[kinds[other]]
        rolled = pltpu.roll(blocks[x], count - 1 if kinds[x] else 1, 0)
        return jnp.where(index == last[kinds[x]], blocks[other][edge : edge + 1], rolled)

    def emit(j, blocks, kinds):
        for x in range(4):
            rows = [(1 + j, blocks[x])]
            if j == cols - 1:
                rows.append((0, before(blocks, x, kinds)))
            if j == 0:
                rows.append((wide - 1, after(blocks, x, kinds)))
            for i, values in rows:
                if kinds[x]:
                    made_turned[x // 2, pl.ds(i, count, stride=wide), :] = values
                else:
                    out_ref[pl.ds(-x % 4 * count * wide + i, count, stride=wide), :] = values

    def turn_over(i):
        return (2 * FIRST + 1 - count - i) % count

    def column(x, j):
        return x_ref[pl.ds(-x % 4 * quarter + j, count, stride=cols), :]

    @pl.when(cut == 0)
    def _():
        for j in range(cols):
            emit(j, [column(x, j) for x in range(4)], (False,) * 4)

    @pl.when(cut != 0)
    def _():
        for x in (1, 3):
            for i in range(count):
                start = -x % 4 * quarter + turn_over(i) * cols
                turned[x // 2, i * cols : (i + 1) * cols, :] = x_ref[start : start + cols, :]
        for j in range(cols):
            a, c = column(0, j), column(2, j)
            b, d = [turned[i, pl.ds(cols - 1 - j, count, stride=cols), :] for i in (0, 1)]
            for parity, (here, mirror) in enumerate(((a + c, d + b), (a - c, d - b))):
                for kind, folded in enumerate((here + mirror, here - mirror)):
                    high, low = halves(folded)
                    part = pl.ds(j * count, count)
                    folds[2 * parity + kind, part, 0:depth] = high
                    folds[2 * parity + kind, part, depth : 2 * depth] = low
        spectra = []
        for i in range(4):
            spectrum = product(table_ref[pl.ds(i * waves, waves), 0 : 2 * quarter], folds[i])
            wave = 2 * lax.broadcasted_iota(jnp.int32, spectrum.shape, 0) + i // 2
            weight = jnp.where(wave == 0, 1.0 / full, 2.0 / full)
            spectrum = jnp.where(wave < cut, spectrum * weight, 0.0)
            spectra.append(jnp.concatenate(halves(spectrum), axis=1))
        step = cols // STEPS
        order = pairs(cols)
        for k in range(STEPS):
            parts = []
            for i in range(4):
                part = pl.ds(4 * waves + i // 2 * quarter + k * step * count, step * count)
                start = i % 2 * BACK_WIDTH
                parts.append(product(table_ref[part, start : start + 2 * waves], spectra[i]))
            made = {}
            for t in range(step):
                ce, se, co, so = [p[t * count : (t + 1) * count] for p in parts]
                j = order[k * step + t]
                made[j, 0], made[cols - 1 - j, 3] = (ce + co) + (se + so), (ce + co) - (se + so)
                made[j, 2], made[cols - 1 - j, 1] = (ce - co) + (se - so), (ce - co) - (se - so)
                if t % 2 == 1:
                    for i in (order[k * step + t - 1], j):
                        emit(i, [made[i, x] for x in range(4)], (False, True, False, True))
        for x in (1, 3):
            for i in range(count):
                start = (-x % 4 * count + turn_over(i)) * wide
                out_ref[start : start + wide, :] = made_turned[x // 2, i * wide : (i + 1) * wide, :]


def stencil_kernel(cols, rows, n_lat, g_ref, cl_ref, ct_ref, cv_ref, out_ref, rim_ref, share_ref, late_ref, made, sems):
    wide = cols + 2
    depth = g_ref.shape[1]
    early = made.shape[0]
    size = early // sems.shape[0]
    lat = lax.axis_index("lat")
    inner = pl.ds(TILE, rows - 2 * TILE)
    lane = lax.broadcasted_iota(jnp.int32, (rows, depth), 1)
    line = lax.broadcasted_iota(jnp.int32, (rows, depth), 0)
    top = lane % LEV == LEV - 1
    bottom = lane % LEV == 0
    flip = jnp.where(lax.broadcasted_iota(jnp.int32, (1, depth), 1) < 2 * LEV, -1.0, 1.0)
    north_sign = jnp.where(lat == 0, flip, 1.0)
    south_sign = jnp.where(lat == n_lat - 1, flip, 1.0)
    coefs = [jnp.transpose(ref[...]) for ref in (cl_ref, ct_ref, cv_ref)]
    line_of = [g_ref[pl.ds(i, rows, stride=wide), :] for i in range(2)]
    copies = []
    for j in range(cols):
        line_of.append(g_ref[pl.ds(j + 2, rows, stride=wide), :])
        west, here, east = line_of[j : j + 3]
        up = jnp.where(line == 0, 0.0, pltpu.roll(here, 1, 0))
        down = jnp.where(line == rows - 1, 0.0, pltpu.roll(here, rows - 1, 0))
        above = jnp.where(top, 0.0, pltpu.roll(here, depth - 1, 1))
        below = jnp.where(bottom, 0.0, pltpu.roll(here, 1, 1))
        twice = 2.0 * here
        lat_share = coefs[1][:, j : j + 1]
        value = (
            here
            + coefs[0][:, j : j + 1] * (east + west - twice)
            + lat_share * (up + down - twice)
            + coefs[2][:, j : j + 1] * (above + below - twice)
        )
        if j < early:
            made[j] = value[TILE : rows - TILE]
        else:
            late_ref[j - early] = value[TILE : rows - TILE]
        rim_ref[0, j] = value[:TILE]
        rim_ref[1, j] = value[rows - TILE :]
        share_ref[0, j] = lat_share[:1] * north_sign
        share_ref[1, j] = lat_share[rows - 1 :] * south_sign
        if j < early and (j + 1) % size == 0:
            part = pl.ds(j + 1 - size, size)
            copies.append(pltpu.make_async_copy(made.at[part], out_ref.at[part, inner], sems.at[j // size]))
            copies[-1].start()
    for copy in copies:
        copy.wait()


def rim_kernel(cols, _, rim_ref, share_ref, late_ref, first_ref, second_ref, out_ref, made, sems):
    rows = out_ref.shape[1]
    late = pl.ds(cols - late_ref.shape[0], late_ref.shape[0])
    copies = [pltpu.make_async_copy(late_ref, out_ref.at[late, pl.ds(TILE, rows - 2 * TILE)], sems.at[2])]
    copies[0].start()
    odd = lax.axis_index("lat") % 2 == 1
    line = lax.broadcasted_iota(jnp.int32, rim_ref.shape[2:], 0)
    for j in range(cols):
        first, second = first_ref[j], second_ref[j]
        north = share_ref[0, j] * jnp.where(odd, second, first)
        south = share_ref[1, j] * jnp.where(odd, first, second)
        made[0, j] = rim_ref[0, j] + jnp.where(line == 0, north, 0.0)
        made[1, j] = rim_ref[1, j] + jnp.where(line == TILE - 1, south, 0.0)
    for edge in (0, 1):
        there = out_ref.at[:, pl.ds(edge * (rows - TILE), TILE)]
        copies.append(pltpu.make_async_copy(made.at[edge], there, sems.at[edge]))
        copies[-1].start()
    for copy in copies:
        copy.wait()


def per_device(fields, cutoff, cap_mask, coef_lon, coef_lat, coef_vert):
    rows, cols, depth = fields.shape
    peers = lax.axis_size("lon")
    n_lat = lax.axis_size("lat")
    vmem = pl.BlockSpec(memory_space=pltpu.VMEM)
    hbm = pl.BlockSpec(memory_space=pltpu.HBM)
    wide = cols + 2

    packed, odd, even = pl.pallas_call(
        pack_kernel,
        out_shape=(
            pltpu.VMEM((rows * cols, depth), jnp.float32),
            pltpu.VMEM((1, 1, depth), jnp.float32),
            pltpu.VMEM((1, 1, depth), jnp.float32),
        ),
        in_specs=[pl.BlockSpec(memory_space=pltpu.HBM)],
        out_specs=(vmem, vmem, vmem),
        scratch_shapes=[pltpu.VMEM((cols, rows, depth), jnp.float32), pltpu.SemaphoreType.DMA((2,))],
        compiler_params=pltpu.CompilerParams(vmem_limit_bytes=4 * MIB),
        cost_estimate=pl.CostEstimate(flops=10000000000, bytes_accessed=67108864, transcendentals=0),
        name="pack",
    )(pltpu.with_memory_space_constraint(jnp.transpose(fields, (1, 0, 2)), pltpu.HBM))
    order = [ring(peers)]
    block = lax.all_to_all(packed.reshape(peers, cols, 1, depth), "lon", 0, 0, axis_index_groups=order, tiled=True)
    table = tables(cols * peers, cols)
    filtered = pl.pallas_call(
        functools.partial(filter_kernel, cols, peers),
        out_shape=jax.ShapeDtypeStruct((peers * wide, depth), jnp.float32),
        in_specs=[vmem] * 4,
        out_specs=vmem,
        scratch_shapes=[
            pltpu.VMEM((4, cols * peers // 4, 2 * depth), jnp.bfloat16),
            pltpu.VMEM((2, cols * peers // 4, depth), jnp.float32),
            pltpu.VMEM((2, wide * peers // 4, depth), jnp.float32),
        ],
        compiler_params=pltpu.CompilerParams(vmem_limit_bytes=16 * MIB),
        name="filter",
    )(
        cutoff,
        cap_mask,
        block.reshape(peers * cols, depth),
        jnp.asarray(table),
    )
    returned = lax.all_to_all(
        filtered.reshape(peers, wide, 1, depth), "lon", 0, 0, axis_index_groups=order, tiled=True
    )
    head, tail = returned[0, 1:-1], returned[-1, 1:-1]
    first, second = [], []
    for lat in range(n_lat):
        for lon in range(peers):
            here = lat * peers + lon
            pair = lat + 1 if lat % 2 else lat - 1
            inside = 0 <= pair < n_lat
            first.append((here, pair * peers + lon if inside else lat * peers + (lon + peers // 2) % peers))
            second.append((here, (lat ^ 1) * peers + lon))
    first = lax.ppermute(odd * tail + even * head, ("lat", "lon"), first)
    second = lax.ppermute(odd * head + even * tail, ("lat", "lon"), second)
    rim_shape = (2, cols, TILE, depth)
    out, rim, share, late = pl.pallas_call(
        functools.partial(stencil_kernel, cols, rows, n_lat),
        out_shape=(
            pltpu.HBM((cols, rows, depth), jnp.float32),
            pltpu.VMEM(rim_shape, jnp.float32),
            pltpu.VMEM((2, cols, 1, depth), jnp.float32),
            pltpu.VMEM((LATE, rows - 2 * TILE, depth), jnp.float32),
        ),
        in_specs=[vmem] * 4,
        out_specs=(hbm, vmem, vmem, vmem),
        scratch_shapes=[
            pltpu.VMEM((cols - LATE, rows - 2 * TILE, depth), jnp.float32),
            pltpu.SemaphoreType.DMA((3,)),
        ],
        compiler_params=pltpu.CompilerParams(vmem_limit_bytes=8 * MIB),
        cost_estimate=pl.CostEstimate(flops=10**9, bytes_accessed=2 * MIB, transcendentals=0),
        name="stencil",
    )(returned.reshape(rows * wide, depth), jnp.transpose(coef_lon), jnp.transpose(coef_lat), jnp.transpose(coef_vert))
    out = pl.pallas_call(
        functools.partial(rim_kernel, cols),
        out_shape=jax.ShapeDtypeStruct((cols, rows, depth), jnp.float32),
        in_specs=[hbm] + [vmem] * 5,
        out_specs=hbm,
        scratch_shapes=[pltpu.VMEM(rim_shape, jnp.float32), pltpu.SemaphoreType.DMA((3,))],
        input_output_aliases={0: 0},
        compiler_params=pltpu.CompilerParams(vmem_limit_bytes=4 * MIB),
        name="rim",
    )(out, rim, share, late, first, second)
    return jnp.transpose(out, (1, 0, 2))


def solution(mesh):
    return jax.shard_map(
        per_device,
        mesh=mesh,
        in_specs=(
            P("lat", "lon", None),
            P(),
            P(),
            P("lat", "lon"),
            P("lat", "lon"),
            P("lat", "lon"),
        ),
        out_specs=P("lat", "lon", None),
        check_vma=False,
    )
```

```python
import functools

import jax
import jax.numpy as jnp
import ml_dtypes
import numpy as np
from jax import lax
from jax.experimental import pallas as pl
from jax.experimental.pallas import tpu as pltpu
from jax.sharding import PartitionSpec as P

LEV = 16
WAVES = 288
BACK_WIDTH = 384
FIRST = 3
STEPS = 1
MIB = 1024 * 1024
TILE = 8
LATE = 12


def pair_table(table, width):
    high = table.astype(ml_dtypes.bfloat16)
    low = (table - high.astype(np.float64)).astype(ml_dtypes.bfloat16)
    blank = np.zeros((table.shape[0], width - 2 * table.shape[1]), ml_dtypes.bfloat16)
    return np.concatenate([high, low, blank], axis=1)


def ring(peers):
    count = peers // 4
    return [q % 4 * count + (FIRST - i) % count for q in range(4) for i in range(count)]


def pairs(cols):
    return [j for i in range(cols // 2) for j in (i, cols - 1 - i)]


def tables(full, cols):
    sectors = np.array(ring(full // cols)[: full // cols // 4])
    forth, back = [], []
    for parity in (0, 1):
        for curve in (np.cos, np.sin):
            for made, columns in ((forth, np.arange(cols)), (back, np.array(pairs(cols)))):
                place = (columns[:, None] + cols * sectors[None, :]).reshape(-1)
                wave = np.arange(parity, WAVES, 2)
                made.append(curve(wave[:, None] * (2 * place[None, :] + 1) % (2 * full) * (np.pi / full)))
    width = 2 * BACK_WIDTH
    below = [np.concatenate([pair_table(m.T, BACK_WIDTH) for m in back[i : i + 2]], axis=1) for i in (0, 2)]
    return np.concatenate([pair_table(m, width) for m in forth] + below, axis=0)


def pack_kernel(x_ref, out_ref, odd_ref, even_ref, held, sems):
    odd = lax.axis_index("lat") % 2 == 1
    odd_ref[...] = jnp.full(odd_ref.shape, jnp.where(odd, 1.0, 0.0), jnp.float32)
    even_ref[...] = jnp.full(even_ref.shape, jnp.where(odd, 0.0, 1.0), jnp.float32)
    cols, rows, _ = x_ref.shape
    parts = sems.shape[0]
    size = cols // parts
    copies = []
    for i in range(parts):
        part = pl.ds(i * size, size)
        copies.append(pltpu.make_async_copy(x_ref.at[part], held.at[part], sems.at[i]))
        copies[-1].start()
    for i in range(parts):
        copies[i].wait()
        for j in range(i * size, (i + 1) * size):
            out_ref[pl.ds(j, rows, stride=cols), :] = held[j]


def halves(values):
    high = values.astype(jnp.bfloat16)
    low = (values - high.astype(jnp.float32)).astype(jnp.bfloat16)
    return high, low


def product(table, data):
    both = jnp.dot(table, jnp.concatenate([data, data], axis=0), preferred_element_type=jnp.float32)
    depth = both.shape[1] // 2
    return both[:, :depth] + both[:, depth:]


def filter_kernel(cols, peers, cut_ref, cap_ref, x_ref, table_ref, out_ref, folds, turned, made_turned):
    depth = x_ref.shape[1]
    full = cols * peers
    count = peers // 4
    wide = cols + 2
    waves = WAVES // 2
    quarter = cols * count
    sector = lax.axis_index("lon")
    turn = sector // count
    row = lax.axis_index("lat") * peers + turn * count + (FIRST + count - sector % count) % count
    line = lax.broadcasted_iota(jnp.int32, (1, cut_ref.shape[0]), 1)
    mine = jnp.where((line == row) & (cap_ref[...].reshape(line.shape) == 1), cut_ref[...].reshape(line.shape), 0)
    cut = jnp.max(mine.astype(jnp.float32)).astype(jnp.int32)
    index = lax.broadcasted_iota(jnp.int32, (count, depth), 0)

    last = {False: (FIRST + 1) % count, True: FIRST}
    first = {False: FIRST, True: (FIRST + 1) % count}

    def before(blocks, x, kinds):
        other = (x - 1) % 4
        edge = last[kinds[other]]
        rolled = pltpu.roll(blocks[x], 1 if kinds[x] else count - 1, 0)
        return jnp.where(index == first[kinds[x]], blocks[other][edge : edge + 1], rolled)

    def after(blocks, x, kinds):
        other = (x + 1) % 4
        edge = first[kinds[other]]
        rolled = pltpu.roll(blocks[x], count - 1 if kinds[x] else 1, 0)
        return jnp.where(index == last[kinds[x]], blocks[other][edge : edge + 1], rolled)

    def emit(j, blocks, kinds):
        for x in range(4):
            rows = [(1 + j, blocks[x])]
            if j == cols - 1:
                rows.append((0, before(blocks, x, kinds)))
            if j == 0:
                rows.append((wide - 1, after(blocks, x, kinds)))
            for i, values in rows:
                if kinds[x]:
                    made_turned[x // 2, pl.ds(i, count, stride=wide), :] = values
                else:
                    out_ref[pl.ds(x % 4 * count * wide + i, count, stride=wide), :] = values

    def turn_over(i):
        return (2 * FIRST + 1 - count - i) % count

    def column(x, j):
        return x_ref[pl.ds(x % 4 * quarter + j, count, stride=cols), :]

    @pl.when(cut == 0)
    def _():
        for j in range(cols):
            emit(j, [column(x, j) for x in range(4)], (False,) * 4)

    @pl.when(cut != 0)
    def _():
        for x in (1, 3):
            for i in range(count):
                start = x % 4 * quarter + turn_over(i) * cols
                turned[x // 2, i * cols : (i + 1) * cols, :] = x_ref[start : start + cols, :]
        for j in range(cols):
            a, c = column(0, j), column(2, j)
            b, d = [turned[i, pl.ds(cols - 1 - j, count, stride=cols), :] for i in (0, 1)]
            for parity, (here, mirror) in enumerate(((a + c, d + b), (a - c, d - b))):
                for kind, folded in enumerate((here + mirror, here - mirror)):
                    high, low = halves(folded)
                    part = pl.ds(j * count, count)
                    folds[2 * parity + kind, part, 0:depth] = high
                    folds[2 * parity + kind, part, depth : 2 * depth] = low
        spectra = []
        for i in range(4):
            spectrum = product(table_ref[pl.ds(i * waves, waves), 0 : 2 * quarter], folds[i])
            wave = 2 * lax.broadcasted_iota(jnp.int32, spectrum.shape, 0) + i // 2
            weight = jnp.where(wave == 0, 1.0 / full, 2.0 / full)
            spectrum = jnp.where(wave < cut, spectrum * weight, 0.0)
            spectra.append(jnp.concatenate(halves(spectrum), axis=1))
        step = cols // STEPS
        order = pairs(cols)
        for k in range(STEPS):
            parts = []
            for i in range(4):
                part = pl.ds(4 * waves + i // 2 * quarter + k * step * count, step * count)
                start = i % 2 * BACK_WIDTH
                parts.append(product(table_ref[part, start : start + 2 * waves], spectra[i]))
            made = {}
            for t in range(step):
                ce, se, co, so = [p[t * count : (t + 1) * count] for p in parts]
                j = order[k * step + t]
                made[j, 0], made[cols - 1 - j, 3] = (ce + co) + (se + so), (ce + co) - (se + so)
                made[j, 2], made[cols - 1 - j, 1] = (ce - co) + (se - so), (ce - co) - (se - so)
                if t % 2 == 1:
                    for i in (order[k * step + t - 1], j):
                        emit(i, [made[i, x] for x in range(4)], (False, True, False, True))
        for x in (1, 3):
            for i in range(count):
                start = (x % 4 * count + turn_over(i)) * wide
                out_ref[start : start + wide, :] = made_turned[x // 2, i * wide : (i + 1) * wide, :]


def stencil_kernel(cols, rows, n_lat, g_ref, cl_ref, ct_ref, cv_ref, out_ref, rim_ref, share_ref, late_ref, made, sems):
    wide = cols + 2
    depth = g_ref.shape[1]
    early = made.shape[0]
    size = early // sems.shape[0]
    lat = lax.axis_index("lat")
    inner = pl.ds(TILE, rows - 2 * TILE)
    lane = lax.broadcasted_iota(jnp.int32, (rows, depth), 1)
    line = lax.broadcasted_iota(jnp.int32, (rows, depth), 0)
    top = lane % LEV == LEV - 1
    bottom = lane % LEV == 0
    flip = jnp.where(lax.broadcasted_iota(jnp.int32, (1, depth), 1) < 2 * LEV, -1.0, 1.0)
    north_sign = jnp.where(lat == 0, flip, 1.0)
    south_sign = jnp.where(lat == n_lat - 1, flip, 1.0)
    coefs = [jnp.transpose(ref[...]) for ref in (cl_ref, ct_ref, cv_ref)]
    line_of = [g_ref[pl.ds(i, rows, stride=wide), :] for i in range(2)]
    copies = []
    for j in range(cols):
        line_of.append(g_ref[pl.ds(j + 2, rows, stride=wide), :])
        west, here, east = line_of[j : j + 3]
        up = jnp.where(line == 0, 0.0, pltpu.roll(here, 1, 0))
        down = jnp.where(line == rows - 1, 0.0, pltpu.roll(here, rows - 1, 0))
        above = jnp.where(top, 0.0, pltpu.roll(here, depth - 1, 1))
        below = jnp.where(bottom, 0.0, pltpu.roll(here, 1, 1))
        twice = 2.0 * here
        lat_share = coefs[1][:, j : j + 1]
        value = (
            here
            + coefs[0][:, j : j + 1] * (east + west - twice)
            + lat_share * (up + down - twice)
            + coefs[2][:, j : j + 1] * (above + below - twice)
        )
        if j < early:
            made[j] = value[TILE : rows - TILE]
        else:
            late_ref[j - early] = value[TILE : rows - TILE]
        rim_ref[0, j] = value[:TILE]
        rim_ref[1, j] = value[rows - TILE :]
        share_ref[0, j] = lat_share[:1] * north_sign
        share_ref[1, j] = lat_share[rows - 1 :] * south_sign
        if j < early and (j + 1) % size == 0:
            part = pl.ds(j + 1 - size, size)
            copies.append(pltpu.make_async_copy(made.at[part], out_ref.at[part, inner], sems.at[j // size]))
            copies[-1].start()
    for copy in copies:
        copy.wait()


def rim_kernel(cols, _, rim_ref, share_ref, late_ref, first_ref, second_ref, out_ref, made, sems):
    rows = out_ref.shape[1]
    late = pl.ds(cols - late_ref.shape[0], late_ref.shape[0])
    copies = [pltpu.make_async_copy(late_ref, out_ref.at[late, pl.ds(TILE, rows - 2 * TILE)], sems.at[2])]
    copies[0].start()
    odd = lax.axis_index("lat") % 2 == 1
    line = lax.broadcasted_iota(jnp.int32, rim_ref.shape[2:], 0)
    for j in range(cols):
        first, second = first_ref[j], second_ref[j]
        north = share_ref[0, j] * jnp.where(odd, second, first)
        south = share_ref[1, j] * jnp.where(odd, first, second)
        made[0, j] = rim_ref[0, j] + jnp.where(line == 0, north, 0.0)
        made[1, j] = rim_ref[1, j] + jnp.where(line == TILE - 1, south, 0.0)
    for edge in (0, 1):
        there = out_ref.at[:, pl.ds(edge * (rows - TILE), TILE)]
        copies.append(pltpu.make_async_copy(made.at[edge], there, sems.at[edge]))
        copies[-1].start()
    for copy in copies:
        copy.wait()


def per_device(fields, cutoff, cap_mask, coef_lon, coef_lat, coef_vert):
    rows, cols, depth = fields.shape
    peers = lax.axis_size("lon")
    n_lat = lax.axis_size("lat")
    vmem = pl.BlockSpec(memory_space=pltpu.VMEM)
    hbm = pl.BlockSpec(memory_space=pltpu.HBM)
    wide = cols + 2

    packed, odd, even = pl.pallas_call(
        pack_kernel,
        out_shape=(
            pltpu.VMEM((rows * cols, depth), jnp.float32),
            pltpu.VMEM((1, 1, depth), jnp.float32),
            pltpu.VMEM((1, 1, depth), jnp.float32),
        ),
        in_specs=[pl.BlockSpec(memory_space=pltpu.HBM)],
        out_specs=(vmem, vmem, vmem),
        scratch_shapes=[pltpu.VMEM((cols, rows, depth), jnp.float32), pltpu.SemaphoreType.DMA((2,))],
        compiler_params=pltpu.CompilerParams(vmem_limit_bytes=4 * MIB),
        cost_estimate=pl.CostEstimate(flops=10000000000, bytes_accessed=67108864, transcendentals=0),
        name="pack",
    )(pltpu.with_memory_space_constraint(jnp.transpose(fields, (1, 0, 2)), pltpu.HBM))
    order = [ring(peers)]
    block = lax.all_to_all(packed.reshape(peers, cols, 1, depth), "lon", 0, 0, axis_index_groups=order, tiled=True)
    table = tables(cols * peers, cols)
    filtered = pl.pallas_call(
        functools.partial(filter_kernel, cols, peers),
        out_shape=jax.ShapeDtypeStruct((peers * wide, depth), jnp.float32),
        in_specs=[vmem] * 4,
        out_specs=vmem,
        scratch_shapes=[
            pltpu.VMEM((4, cols * peers // 4, 2 * depth), jnp.bfloat16),
            pltpu.VMEM((2, cols * peers // 4, depth), jnp.float32),
            pltpu.VMEM((2, wide * peers // 4, depth), jnp.float32),
        ],
        compiler_params=pltpu.CompilerParams(vmem_limit_bytes=16 * MIB),
        name="filter",
    )(
        cutoff,
        cap_mask,
        block.reshape(peers * cols, depth),
        jnp.asarray(table),
    )
    returned = lax.all_to_all(
        filtered.reshape(peers, wide, 1, depth), "lon", 0, 0, axis_index_groups=order, tiled=True
    )
    head, tail = returned[0, 1:-1], returned[-1, 1:-1]
    first, second = [], []
    for lat in range(n_lat):
        for lon in range(peers):
            here = lat * peers + lon
            pair = lat + 1 if lat % 2 else lat - 1
            inside = 0 <= pair < n_lat
            first.append((here, pair * peers + lon if inside else lat * peers + (lon + peers // 2) % peers))
            second.append((here, (lat ^ 1) * peers + lon))
    first = lax.ppermute(odd * tail + even * head, ("lat", "lon"), first)
    second = lax.ppermute(odd * head + even * tail, ("lat", "lon"), second)
    rim_shape = (2, cols, TILE, depth)
    out, rim, share, late = pl.pallas_call(
        functools.partial(stencil_kernel, cols, rows, n_lat),
        out_shape=(
            pltpu.HBM((cols, rows, depth), jnp.float32),
            pltpu.VMEM(rim_shape, jnp.float32),
            pltpu.VMEM((2, cols, 1, depth), jnp.float32),
            pltpu.VMEM((LATE, rows - 2 * TILE, depth), jnp.float32),
        ),
        in_specs=[vmem] * 4,
        out_specs=(hbm, vmem, vmem, vmem),
        scratch_shapes=[
            pltpu.VMEM((cols - LATE, rows - 2 * TILE, depth), jnp.float32),
            pltpu.SemaphoreType.DMA((3,)),
        ],
        compiler_params=pltpu.CompilerParams(vmem_limit_bytes=8 * MIB),
        cost_estimate=pl.CostEstimate(flops=10**9, bytes_accessed=2 * MIB, transcendentals=0),
        name="stencil",
    )(returned.reshape(rows * wide, depth), jnp.transpose(coef_lon), jnp.transpose(coef_lat), jnp.transpose(coef_vert))
    out = pl.pallas_call(
        functools.partial(rim_kernel, cols),
        out_shape=jax.ShapeDtypeStruct((cols, rows, depth), jnp.float32),
        in_specs=[hbm] + [vmem] * 5,
        out_specs=hbm,
        scratch_shapes=[pltpu.VMEM(rim_shape, jnp.float32), pltpu.SemaphoreType.DMA((3,))],
        input_output_aliases={0: 0},
        compiler_params=pltpu.CompilerParams(vmem_limit_bytes=4 * MIB),
        name="rim",
    )(out, rim, share, late, first, second)
    return jnp.transpose(out, (1, 0, 2))


def solution(mesh):
    return jax.shard_map(
        per_device,
        mesh=mesh,
        in_specs=(
            P("lat", "lon", None),
            P(),
            P(),
            P("lat", "lon"),
            P("lat", "lon"),
            P("lat", "lon"),
        ),
        out_specs=P("lat", "lon", None),
        check_vma=False,
    )
```

```python
import functools

import jax
import jax.numpy as jnp
import ml_dtypes
import numpy as np
from jax import lax
from jax.experimental import pallas as pl
from jax.experimental.pallas import tpu as pltpu
from jax.sharding import PartitionSpec as P

LEV = 16
WAVES = 288
BACK_WIDTH = 384
FIRST = 3
STEPS = 1
MIB = 1024 * 1024
TILE = 8
LATE = 9


def pair_table(table, width):
    high = table.astype(ml_dtypes.bfloat16)
    low = (table - high.astype(np.float64)).astype(ml_dtypes.bfloat16)
    blank = np.zeros((table.shape[0], width - 2 * table.shape[1]), ml_dtypes.bfloat16)
    return np.concatenate([high, low, blank], axis=1)


def ring(peers):
    count = peers // 4
    return [q * count + (FIRST - i) % count for q in range(4) for i in range(count)]


def pairs(cols):
    return [j for i in range(cols // 2) for j in (i, cols - 1 - i)]


def tables(full, cols):
    sectors = np.array(ring(full // cols)[: full // cols // 4])
    forth, back = [], []
    for parity in (0, 1):
        for curve in (np.cos, np.sin):
            for made, columns in ((forth, np.arange(cols)), (back, np.array(pairs(cols)))):
                place = (columns[:, None] + cols * sectors[None, :]).reshape(-1)
                wave = np.arange(parity, WAVES, 2)
                made.append(curve(wave[:, None] * (2 * place[None, :] + 1) % (2 * full) * (np.pi / full)))
    width = 2 * BACK_WIDTH
    below = [np.concatenate([pair_table(m.T, BACK_WIDTH) for m in back[i : i + 2]], axis=1) for i in (0, 2)]
    return np.concatenate([pair_table(m, width) for m in forth] + below, axis=0)


def pack_kernel(x_ref, out_ref, odd_ref, even_ref, held, sems):
    odd = lax.axis_index("lat") % 2 == 1
    odd_ref[...] = jnp.full(odd_ref.shape, jnp.where(odd, 1.0, 0.0), jnp.float32)
    even_ref[...] = jnp.full(even_ref.shape, jnp.where(odd, 0.0, 1.0), jnp.float32)
    cols, rows, _ = x_ref.shape
    parts = sems.shape[0]
    size = cols // parts
    copies = []
    for i in range(parts):
        part = pl.ds(i * size, size)
        copies.append(pltpu.make_async_copy(x_ref.at[part], held.at[part], sems.at[i]))
        copies[-1].start()
    for i in range(parts):
        copies[i].wait()
        for j in range(i * size, (i + 1) * size):
            out_ref[pl.ds(j, rows, stride=cols), :] = held[j]


def halves(values):
    high = values.astype(jnp.bfloat16)
    low = (values - high.astype(jnp.float32)).astype(jnp.bfloat16)
    return high, low


def product(table, data):
    both = jnp.dot(table, jnp.concatenate([data, data], axis=0), preferred_element_type=jnp.float32)
    depth = both.shape[1] // 2
    return both[:, :depth] + both[:, depth:]


def filter_kernel(cols, peers, cut_ref, cap_ref, x_ref, table_ref, out_ref, folds, turned, made_turned):
    depth = x_ref.shape[1]
    full = cols * peers
    count = peers // 4
    wide = cols + 2
    waves = WAVES // 2
    quarter = cols * count
    sector = lax.axis_index("lon")
    turn = sector // count
    row = lax.axis_index("lat") * peers + turn * count + (FIRST + count - sector % count) % count
    line = lax.broadcasted_iota(jnp.int32, (1, cut_ref.shape[0]), 1)
    mine = jnp.where((line == row) & (cap_ref[...].reshape(line.shape) == 1), cut_ref[...].reshape(line.shape), 0)
    cut = jnp.max(mine.astype(jnp.float32)).astype(jnp.int32)
    index = lax.broadcasted_iota(jnp.int32, (count, depth), 0)

    last = {False: (FIRST + 1) % count, True: FIRST}
    first = {False: FIRST, True: (FIRST + 1) % count}

    def before(blocks, x, kinds):
        other = (x - 1) % 4
        edge = last[kinds[other]]
        rolled = pltpu.roll(blocks[x], 1 if kinds[x] else count - 1, 0)
        return jnp.where(index == first[kinds[x]], blocks[other][edge : edge + 1], rolled)

    def after(blocks, x, kinds):
        other = (x + 1) % 4
        edge = first[kinds[other]]
        rolled = pltpu.roll(blocks[x], count - 1 if kinds[x] else 1, 0)
        return jnp.where(index == last[kinds[x]], blocks[other][edge : edge + 1], rolled)

    def emit(j, blocks, kinds):
        for x in range(4):
            rows = [(1 + j, blocks[x])]
            if j == cols - 1:
                rows.append((0, before(blocks, x, kinds)))
            if j == 0:
                rows.append((wide - 1, after(blocks, x, kinds)))
            for i, values in rows:
                if kinds[x]:
                    made_turned[x // 2, pl.ds(i, count, stride=wide), :] = values
                else:
                    out_ref[pl.ds(x * count * wide + i, count, stride=wide), :] = values

    def turn_over(i):
        return (2 * FIRST + 1 - count - i) % count

    def column(x, j):
        return x_ref[pl.ds(x * quarter + j, count, stride=cols), :]

    @pl.when(cut == 0)
    def _():
        for j in range(cols):
            emit(j, [column(x, j) for x in range(4)], (False,) * 4)

    @pl.when(cut != 0)
    def _():
        for x in (1, 3):
            for i in range(count):
                start = x * quarter + turn_over(i) * cols
                turned[x // 2, i * cols : (i + 1) * cols, :] = x_ref[start : start + cols, :]
        for j in range(cols):
            a, c = column(0, j), column(2, j)
            b, d = [turned[i, pl.ds(cols - 1 - j, count, stride=cols), :] for i in (0, 1)]
            for parity, (here, mirror) in enumerate(((a + c, d + b), (a - c, d - b))):
                for kind, folded in enumerate((here + mirror, here - mirror)):
                    high, low = halves(folded)
                    part = pl.ds(j * count, count)
                    folds[2 * parity + kind, part, 0:depth] = high
                    folds[2 * parity + kind, part, depth : 2 * depth] = low
        spectra = []
        for i in range(4):
            spectrum = product(table_ref[pl.ds(i * waves, waves), 0 : 2 * quarter], folds[i])
            wave = 2 * lax.broadcasted_iota(jnp.int32, spectrum.shape, 0) + i // 2
            weight = jnp.where(wave == 0, 1.0 / full, 2.0 / full)
            spectrum = jnp.where(wave < cut, spectrum * weight, 0.0)
            spectra.append(jnp.concatenate(halves(spectrum), axis=1))
        step = cols // STEPS
        order = pairs(cols)
        for k in range(STEPS):
            parts = []
            for i in range(4):
                part = pl.ds(4 * waves + i // 2 * quarter + k * step * count, step * count)
                start = i % 2 * BACK_WIDTH
                parts.append(product(table_ref[part, start : start + 2 * waves], spectra[i]))
            made = {}
            for t in range(step):
                ce, se, co, so = [p[t * count : (t + 1) * count] for p in parts]
                j = order[k * step + t]
                made[j, 0], made[cols - 1 - j, 3] = (ce + co) + (se + so), (ce + co) - (se + so)
                made[j, 2], made[cols - 1 - j, 1] = (ce - co) + (se - so), (ce - co) - (se - so)
                if t % 2 == 1:
                    for i in (order[k * step + t - 1], j):
                        emit(i, [made[i, x] for x in range(4)], (False, True, False, True))
        for x in (1, 3):
            for i in range(count):
                start = (x * count + turn_over(i)) * wide
                out_ref[start : start + wide, :] = made_turned[x // 2, i * wide : (i + 1) * wide, :]


def stencil_kernel(cols, rows, n_lat, g_ref, cl_ref, ct_ref, cv_ref, out_ref, rim_ref, share_ref, late_ref, made, sems):
    wide = cols + 2
    depth = g_ref.shape[1]
    early = made.shape[0]
    size = early // sems.shape[0]
    lat = lax.axis_index("lat")
    inner = pl.ds(TILE, rows - 2 * TILE)
    lane = lax.broadcasted_iota(jnp.int32, (rows, depth), 1)
    line = lax.broadcasted_iota(jnp.int32, (rows, depth), 0)
    top = lane % LEV == LEV - 1
    bottom = lane % LEV == 0
    flip = jnp.where(lax.broadcasted_iota(jnp.int32, (1, depth), 1) < 2 * LEV, -1.0, 1.0)
    north_sign = jnp.where(lat == 0, flip, 1.0)
    south_sign = jnp.where(lat == n_lat - 1, flip, 1.0)
    coefs = [jnp.transpose(ref[...]) for ref in (cl_ref, ct_ref, cv_ref)]
    line_of = [g_ref[pl.ds(i, rows, stride=wide), :] for i in range(2)]
    copies = []
    for j in range(cols):
        line_of.append(g_ref[pl.ds(j + 2, rows, stride=wide), :])
        west, here, east = line_of[j : j + 3]
        up = jnp.where(line == 0, 0.0, pltpu.roll(here, 1, 0))
        down = jnp.where(line == rows - 1, 0.0, pltpu.roll(here, rows - 1, 0))
        above = jnp.where(top, 0.0, pltpu.roll(here, depth - 1, 1))
        below = jnp.where(bottom, 0.0, pltpu.roll(here, 1, 1))
        twice = 2.0 * here
        lat_share = coefs[1][:, j : j + 1]
        value = (
            here
            + coefs[0][:, j : j + 1] * (east + west - twice)
            + lat_share * (up + down - twice)
            + coefs[2][:, j : j + 1] * (above + below - twice)
        )
        if j < early:
            made[j] = value[TILE : rows - TILE]
        else:
            late_ref[j - early] = value[TILE : rows - TILE]
        rim_ref[0, j] = value[:TILE]
        rim_ref[1, j] = value[rows - TILE :]
        share_ref[0, j] = lat_share[:1] * north_sign
        share_ref[1, j] = lat_share[rows - 1 :] * south_sign
        if j < early and (j + 1) % size == 0:
            part = pl.ds(j + 1 - size, size)
            copies.append(pltpu.make_async_copy(made.at[part], out_ref.at[part, inner], sems.at[j // size]))
            copies[-1].start()
    for copy in copies:
        copy.wait()


def rim_kernel(cols, _, rim_ref, share_ref, late_ref, first_ref, second_ref, out_ref, made, sems):
    rows = out_ref.shape[1]
    late = pl.ds(cols - late_ref.shape[0], late_ref.shape[0])
    copies = [pltpu.make_async_copy(late_ref, out_ref.at[late, pl.ds(TILE, rows - 2 * TILE)], sems.at[2])]
    copies[0].start()
    odd = lax.axis_index("lat") % 2 == 1
    line = lax.broadcasted_iota(jnp.int32, rim_ref.shape[2:], 0)
    for j in range(cols):
        first, second = first_ref[j], second_ref[j]
        north = share_ref[0, j] * jnp.where(odd, second, first)
        south = share_ref[1, j] * jnp.where(odd, first, second)
        made[0, j] = rim_ref[0, j] + jnp.where(line == 0, north, 0.0)
        made[1, j] = rim_ref[1, j] + jnp.where(line == TILE - 1, south, 0.0)
    for edge in (0, 1):
        there = out_ref.at[:, pl.ds(edge * (rows - TILE), TILE)]
        copies.append(pltpu.make_async_copy(made.at[edge], there, sems.at[edge]))
        copies[-1].start()
    for copy in copies:
        copy.wait()


def per_device(fields, cutoff, cap_mask, coef_lon, coef_lat, coef_vert):
    rows, cols, depth = fields.shape
    peers = lax.axis_size("lon")
    n_lat = lax.axis_size("lat")
    vmem = pl.BlockSpec(memory_space=pltpu.VMEM)
    hbm = pl.BlockSpec(memory_space=pltpu.HBM)
    wide = cols + 2

    packed, odd, even = pl.pallas_call(
        pack_kernel,
        out_shape=(
            pltpu.VMEM((rows * cols, depth), jnp.float32),
            pltpu.VMEM((1, 1, depth), jnp.float32),
            pltpu.VMEM((1, 1, depth), jnp.float32),
        ),
        in_specs=[pl.BlockSpec(memory_space=pltpu.HBM)],
        out_specs=(vmem, vmem, vmem),
        scratch_shapes=[pltpu.VMEM((cols, rows, depth), jnp.float32), pltpu.SemaphoreType.DMA((2,))],
        compiler_params=pltpu.CompilerParams(vmem_limit_bytes=4 * MIB),
        cost_estimate=pl.CostEstimate(flops=10000000000, bytes_accessed=67108864, transcendentals=0),
        name="pack",
    )(pltpu.with_memory_space_constraint(jnp.transpose(fields, (1, 0, 2)), pltpu.HBM))
    order = [ring(peers)]
    block = lax.all_to_all(packed.reshape(peers, cols, 1, depth), "lon", 0, 0, axis_index_groups=order, tiled=True)
    table = tables(cols * peers, cols)
    filtered = pl.pallas_call(
        functools.partial(filter_kernel, cols, peers),
        out_shape=jax.ShapeDtypeStruct((peers * wide, depth), jnp.float32),
        in_specs=[vmem] * 4,
        out_specs=vmem,
        scratch_shapes=[
            pltpu.VMEM((4, cols * peers // 4, 2 * depth), jnp.bfloat16),
            pltpu.VMEM((2, cols * peers // 4, depth), jnp.float32),
            pltpu.VMEM((2, wide * peers // 4, depth), jnp.float32),
        ],
        compiler_params=pltpu.CompilerParams(vmem_limit_bytes=16 * MIB),
        name="filter",
    )(
        cutoff,
        cap_mask,
        block.reshape(peers * cols, depth),
        jnp.asarray(table),
    )
    returned = lax.all_to_all(
        filtered.reshape(peers, wide, 1, depth), "lon", 0, 0, axis_index_groups=order, tiled=True
    )
    head, tail = returned[0, 1:-1], returned[-1, 1:-1]
    first, second = [], []
    for lat in range(n_lat):
        for lon in range(peers):
            here = lat * peers + lon
            pair = lat + 1 if lat % 2 else lat - 1
            inside = 0 <= pair < n_lat
            first.append((here, pair * peers + lon if inside else lat * peers + (lon + peers // 2) % peers))
            second.append((here, (lat ^ 1) * peers + lon))
    first = lax.ppermute(odd * tail + even * head, ("lat", "lon"), first)
    second = lax.ppermute(odd * head + even * tail, ("lat", "lon"), second)
    rim_shape = (2, cols, TILE, depth)
    out, rim, share, late = pl.pallas_call(
        functools.partial(stencil_kernel, cols, rows, n_lat),
        out_shape=(
            pltpu.HBM((cols, rows, depth), jnp.float32),
            pltpu.VMEM(rim_shape, jnp.float32),
            pltpu.VMEM((2, cols, 1, depth), jnp.float32),
            pltpu.VMEM((LATE, rows - 2 * TILE, depth), jnp.float32),
        ),
        in_specs=[vmem] * 4,
        out_specs=(hbm, vmem, vmem, vmem),
        scratch_shapes=[
            pltpu.VMEM((cols - LATE, rows - 2 * TILE, depth), jnp.float32),
            pltpu.SemaphoreType.DMA((3,)),
        ],
        compiler_params=pltpu.CompilerParams(vmem_limit_bytes=8 * MIB),
        cost_estimate=pl.CostEstimate(flops=10**9, bytes_accessed=2 * MIB, transcendentals=0),
        name="stencil",
    )(returned.reshape(rows * wide, depth), jnp.transpose(coef_lon), jnp.transpose(coef_lat), jnp.transpose(coef_vert))
    out = pl.pallas_call(
        functools.partial(rim_kernel, cols),
        out_shape=jax.ShapeDtypeStruct((cols, rows, depth), jnp.float32),
        in_specs=[hbm] + [vmem] * 5,
        out_specs=hbm,
        scratch_shapes=[pltpu.VMEM(rim_shape, jnp.float32), pltpu.SemaphoreType.DMA((3,))],
        input_output_aliases={0: 0},
        compiler_params=pltpu.CompilerParams(vmem_limit_bytes=4 * MIB),
        name="rim",
    )(out, rim, share, late, first, second)
    return jnp.transpose(out, (1, 0, 2))


def solution(mesh):
    return jax.shard_map(
        per_device,
        mesh=mesh,
        in_specs=(
            P("lat", "lon", None),
            P(),
            P(),
            P("lat", "lon"),
            P("lat", "lon"),
            P("lat", "lon"),
        ),
        out_specs=P("lat", "lon", None),
        check_vma=False,
    )
```
